32 devices in a mesh: layer: 4 (over y, core), tx: 2 (over x), ty: 4 (over z).
Axes of the slice: x: 2, y: 2, z: 4, core: 2. Of those that a mesh axis runs over, the one named last changes fastest.
Arguments:
- layers: float32 [4, 256, 2048], P('layer', 'tx', 'ty'), may hold values from -6 to 6
- wind: int32 [4, 2], P('layer'), may hold values from -128 to 128
- offsets: int32 [4, 9, 2], P('layer'), may hold values from -64 to 64
- weights: bfloat16 [9, 2, 256, 2048], P(None, None, 'tx', 'ty'), may hold values from -0.5 to 0.5
- sub_index: int32 [256, 2048], P('tx', 'ty'), may hold values from -1 to 255, as said below
Outputs:
- slopes: float32 [2, 9, 32, 256], P(None, None, 'tx', 'ty')
The draws below stay inside these ranges and needn't reach their ends.
Inputs may be any that keep to these rules, and one draw needn't show every extreme that they name: sub_index[i, j] is -1 or j // 8.
All inputs are finite; a program needn't handle non-finite values.
Results may differ from the reference program's by a relative error of at most 0.0003.
Values sent between devices are 32-bit elements; how exact they have to be, the bound alone decides.
A program may use at most 256 MiB of HBM per device.

```python
import jax
import jax.numpy as jnp
from jax import lax

DIRS = 9
SUB = 8
HMAX = 2
FOOT = 64
LAYERS = 4
NX = 256
NY = 2048


def draw_wind(key, part):
    key_a, key_b, key_c = jax.random.split(jax.random.fold_in(key, 11), 3)
    top = 64 * HMAX
    base = jax.random.randint(key_a, (LAYERS, 2), -top, top + 1)
    high = jax.random.randint(key_b, (1, 2), 0, LAYERS)
    low = (high + 1 + jax.random.randint(key_c, (1, 2), 0, LAYERS - 1)) % LAYERS
    rows = jnp.arange(LAYERS)[:, None]
    base = jnp.where(rows == high, top, base)
    base = jnp.where(rows == low, -top, base)
    return base.astype(jnp.int32)


def draw_offsets(key, part):
    key_a, key_b, key_c = jax.random.split(jax.random.fold_in(key, 23), 3)
    base = jax.random.randint(key_a, (LAYERS, DIRS, 2), -FOOT, FOOT + 1)
    high = jax.random.randint(key_b, (LAYERS, 1, 2), 0, DIRS)
    low = (high + 1 + jax.random.randint(key_c, (LAYERS, 1, 2), 0, DIRS - 1)) % DIRS
    dirs = jnp.arange(DIRS)[None, :, None]
    base = jnp.where(dirs == high, FOOT, base)
    base = jnp.where(dirs == low, -FOOT, base)
    return base.astype(jnp.int32)


def draw_sub_index(key, part):
    rows = jnp.arange(NX)[:, None]
    cols = jnp.arange(NY)[None, :]
    column = jnp.broadcast_to(cols // SUB, (NX, NY))
    dead = jax.random.randint(jax.random.fold_in(key, 37), (NX, NY), 0, 8) == 0
    corner_first = (rows == 0) & (cols == 0)
    corner_last = (rows == NX - 1) & (cols == NY - 1)
    dead = (dead | corner_first) & jnp.logical_not(corner_last)
    return jnp.where(dead, -1, column).astype(jnp.int32)


def shard_levels(own_key, shape, cuts, least, largest):
    def one(axis_at, shards_of):
        draws = jax.random.uniform(jax.random.fold_in(jax.random.fold_in(own_key, 6), axis_at), (shards_of,), jnp.float32, least / len(cuts), largest / len(cuts))
        return jnp.repeat(jnp.exp(draws), shape[axis_at] // shards_of).reshape((-1,) + (1,) * (len(shape) - axis_at - 1))

    gain = one(*cuts[0])
    for cut in cuts[1:]:
        gain = gain * one(*cut)
    return gain


def scatter_about(stream_key, dims, scale, limit, cuts=(), dtype=jnp.bfloat16):
    array = jax.random.normal(stream_key, dims, jnp.float32) * scale
    if len(cuts) > 0:
        array = shard_levels(stream_key, dims, cuts, -0.22, 0.18) * array
    return jnp.clip(array, min=-limit, max=limit).astype(dtype)


def setup_inputs(seed: int = 0) -> dict:
    key_of = jax.random.split(jax.random.key(seed), 6)
    layers = scatter_about(key_of[0], (LAYERS, NX, NY), 1.0, 6.0, ((0, 4), (1, 2), (2, 4)), jnp.float32)
    wind = draw_wind(jax.random.fold_in(key_of[5], 71), 0)
    offsets = draw_offsets(jax.random.fold_in(key_of[5], 71), 0)
    weights = scatter_about(key_of[3], (DIRS, 2, NX, NY), 0.03125, 0.5, ((2, 2), (3, 4)))
    sub_index = draw_sub_index(jax.random.fold_in(key_of[5], 71), 0)
    return dict(layers=layers, wind=wind, offsets=offsets, weights=weights, sub_index=sub_index)


def reference(layers, wind, offsets, weights, sub_index):
    quotient = jnp.floor_divide(wind, 64).astype(jnp.int32)
    fraction = (wind - 64 * quotient).astype(jnp.float32) / 64.0
    live = (sub_index >= 0).astype(jnp.float32)

    def one_layer(total, item):
        field, whole, part, moves = item
        qrow = whole[0]
        qcol = whole[1]
        frow = part[0]
        fcol = part[1]
        corner_aa = jnp.roll(field, (qrow, qcol), (0, 1))
        corner_ab = jnp.roll(field, (qrow, qcol + 1), (0, 1))
        corner_ba = jnp.roll(field, (qrow + 1, qcol), (0, 1))
        corner_bb = jnp.roll(field, (qrow + 1, qcol + 1), (0, 1))
        shifted = (1.0 - frow) * ((1.0 - fcol) * corner_aa + fcol * corner_ab) + frow * ((1.0 - fcol) * corner_ba + fcol * corner_bb)
        views = jnp.stack([jnp.roll(shifted, (-moves[d, 0], -moves[d, 1]), (0, 1)) for d in range(DIRS)])
        return total + views, None

    start = jnp.zeros((DIRS, NX, NY), jnp.float32)
    total, _ = lax.scan(one_layer, start, (layers, quotient, fraction, offsets))
    masked = total * live
    terms = weights.astype(jnp.float32) * masked[:, None]
    sums = terms.reshape(DIRS, 2, NX // SUB, SUB, NY // SUB, SUB).sum(axis=(3, 5))
    return jnp.transpose(sums, (1, 0, 2, 3))
```

```python
import functools

import jax
import jax.numpy as jnp
from jax import lax
from jax.experimental import pallas as pl
from jax.experimental.pallas import tpu as pltpu
from jax.sharding import PartitionSpec as P

DIRS = 9
SUB = 8
HMAX = 2
FOOT = 64
LANES = 128
RIM = 72
MESH = pl.DeviceIdType.MESH


def kernel(
    sizes, wind_hbm, offsets_hbm, layers, weights, sub_index, out, wind, offsets, small_sem, field, shifted, wraw, wlive, sub, parts,
    local_sem, xs_sem, xr_sem, zs_sem, zr_sem, ss_sem, sr_sem,
):
    n_layer, n_tx, n_ty = sizes
    rows, cols = sub_index.shape
    tiles = cols // LANES
    groups = rows // SUB
    last = tiles + 1
    foot_rows = RIM if n_tx > 2 else rows - RIM
    layer = lax.axis_index("layer")
    tx = lax.axis_index("tx")
    ty = lax.axis_index("ty")
    up = {"tx": lax.rem(tx + n_tx - 1, n_tx)}
    down = {"tx": lax.rem(tx + 1, n_tx)}
    left = {"ty": lax.rem(ty + n_ty - 1, n_ty)}
    right = {"ty": lax.rem(ty + 1, n_ty)}
    peers = [{"layer": lax.rem(layer + k, n_layer)} for k in range(1, n_layer)]

    small = [pltpu.make_async_copy(wind_hbm, wind, small_sem.at[0]), pltpu.make_async_copy(offsets_hbm, offsets, small_sem.at[1])]
    for copy in small:
        copy.start()
    order = [0, tiles - 1] + list(range(1, tiles - 1))
    own = {}
    for c in order:
        copy = pltpu.make_async_copy(
            layers.at[0, :, pl.ds(c * LANES, LANES)],
            field.at[c + 1, pl.ds(RIM, rows), :],
            local_sem.at[c],
        )
        copy.start()
        own[c] = copy
    sub_copy = pltpu.make_async_copy(sub_index, sub, local_sem.at[tiles])
    sub_copy.start()
    weight_copy = pltpu.make_async_copy(weights, wraw, local_sem.at[tiles + 1])
    weight_copy.start()

    barrier = pltpu.get_barrier_semaphore()
    greeted = [up, left, right] if n_tx == 2 else [up, down, left, right]
    for device in greeted + peers:
        pl.semaphore_signal(barrier, inc=1, device_id=device, device_id_type=MESH)
    pl.semaphore_wait(barrier, len(greeted) + len(peers))

    def send(src, dst, send_sem, recv_sem, device):
        copy = pltpu.make_async_remote_copy(
            src_ref=src, dst_ref=dst, send_sem=send_sem, recv_sem=recv_sem,
            device_id=device, device_id_type=MESH,
        )
        copy.start()
        return copy

    def send_rows(c):
        return [
            send(
                field.at[c, pl.ds(rows, RIM), :], field.at[c, pl.ds(0, RIM), :],
                xs_sem.at[c - 1, 0], xr_sem.at[c - 1, 0], down,
            ),
            send(
                field.at[c, pl.ds(RIM, foot_rows), :], field.at[c, pl.ds(RIM + rows, foot_rows), :],
                xs_sem.at[c - 1, 1], xr_sem.at[c - 1, 1], up,
            ),
        ]

    def send_cols(start, size, k):
        return [
            send(
                field.at[tiles, pl.ds(start, size), :], field.at[0, pl.ds(start, size), :],
                zs_sem.at[0, k], zr_sem.at[0, k], right,
            ),
            send(
                field.at[1, pl.ds(start, size), :], field.at[last, pl.ds(start, size), :],
                zs_sem.at[1, k], zr_sem.at[1, k], left,
            ),
        ]

    edge_copies, mid_copies = [], []
    for c in order[:2]:
        own[c].wait()
        edge_copies += send_rows(c + 1)
    col_copies = send_cols(RIM, rows, 0)
    for c in order[2:]:
        own[c].wait()
        mid_copies += send_rows(c + 1)

    sub_copy.wait()
    weight_copy.wait()
    for copy in small:
        copy.wait()

    def prepare(d, carry):
        for c in range(tiles):
            for g in range(0, groups, 2):
                live = (sub[pl.ds(g * SUB, 2 * SUB), pl.ds(c * LANES, LANES)] >= 0).astype(jnp.float32)
                for s in range(2):
                    both = wraw[d, s, pl.ds(g * SUB, 2 * SUB), pl.ds(c * LANES, LANES)].astype(jnp.float32) * live
                    for h in range(2):
                        wlive[d, s, c, pl.ds(g + h, SUB, stride=groups), :] = both[h * SUB : (h + 1) * SUB]
        return carry

    lax.fori_loop(0, 4, prepare, 0)
    for copy in edge_copies:
        copy.wait_recv()
    col_copies += send_cols(0, RIM, 1) + send_cols(RIM + rows, foot_rows, 2)
    lax.fori_loop(4, DIRS, prepare, 0)

    for copy in mid_copies:
        copy.wait_recv()
    for copy in col_copies:
        copy.wait_recv()
    if n_tx == 2:
        for c in range(tiles + 2):
            field[c, pl.ds(RIM + rows + foot_rows, RIM - foot_rows), :] = field[c, pl.ds(0, RIM - foot_rows), :]

    wide = rows // SUB + 2 * FOOT // SUB
    qrow = lax.shift_right_arithmetic(wind[0, 0], 6)
    qcol = lax.shift_right_arithmetic(wind[0, 1], 6)
    frow = (wind[0, 0] - 64 * qrow).astype(jnp.float32) / 64.0
    fcol = (wind[0, 1] - 64 * qcol).astype(jnp.float32) / 64.0
    lead = HMAX + 1 - qcol
    lane = lax.broadcasted_iota(jnp.int32, (wide, LANES), 1)

    def shift_phase(p, carry):
        mixed = []
        for c in range(tiles + 2):
            here = field[c, pl.ds(RIM - FOOT + p - qrow, wide, stride=SUB), :]
            above = field[c, pl.ds(RIM - FOOT - 1 + p - qrow, wide, stride=SUB), :]
            mixed.append((1.0 - frow) * here + frow * above)
        first = [pltpu.roll(m, (LANES - lead) & (LANES - 1), 1) for m in mixed]
        second = [pltpu.roll(m, (LANES + 1 - lead) & (LANES - 1), 1) for m in mixed]
        for c in range(tiles + 2):
            after = min(c + 1, last)
            one = jnp.where(lane < LANES - lead, first[c], first[after])
            two = jnp.where(lane < LANES + 1 - lead, second[c], second[after])
            shifted[c, p, :, :] = (1.0 - fcol) * one + fcol * two
        return carry

    lax.fori_loop(0, SUB, shift_phase, 0)

    lane_g = lax.broadcasted_iota(jnp.int32, (groups, LANES), 1)
    half = cols // SUB
    pick_row = lax.broadcasted_iota(jnp.int32, (cols, LANES), 0)
    pick_col = lax.broadcasted_iota(jnp.int32, (cols, LANES), 1)
    pick = (lax.shift_right_logical(pick_row, 3) == (pick_col & (half - 1))).astype(jnp.bfloat16)

    def slopes(d, carry):
        top = offsets[0, 0, d] + FOOT
        begin = offsets[0, 1, d] + LANES - HMAX - 1
        base = lax.shift_right_arithmetic(begin, 7)
        skip = begin & (LANES - 1)
        turn = (LANES - skip) & (LANES - 1)
        sums = [[None] * tiles for _ in range(2)]
        for r in range(SUB):
            row = top + r
            phase = row & (SUB - 1)
            first = lax.shift_right_arithmetic(row, 3)
            turned = [
                pltpu.roll(shifted[base + c, phase, pl.ds(first, groups), :], turn, 1) for c in range(tiles + 1)
            ]
            for c in range(tiles):
                view = jnp.where(lane_g < LANES - skip, turned[c], turned[c + 1])
                for s in range(2):
                    term = wlive[d, s, c, pl.ds(r * groups, groups), :] * view
                    sums[s][c] = term if r == 0 else sums[s][c] + term
        rows_of = []
        for s in range(2):
            total = jnp.concatenate(sums[s], axis=1)
            high = total.astype(jnp.bfloat16)
            low = (total - high.astype(jnp.float32)).astype(jnp.bfloat16)
            rows_of += [high, low]
        added = jnp.dot(jnp.concatenate(rows_of, axis=0), pick, preferred_element_type=jnp.float32)
        one = added[0:groups] + added[groups : 2 * groups]
        two = added[2 * groups : 3 * groups] + added[3 * groups : 4 * groups]
        parts[layer, d, :, :] = jnp.where(lane_g < half, one, two)
        return carry

    sum_copies = []
    cuts = [0, 4, 7, DIRS]
    for b in range(3):
        lax.fori_loop(cuts[b], cuts[b + 1], slopes, 0)
        for k in range(n_layer - 1):
            block = parts.at[layer, pl.ds(cuts[b], cuts[b + 1] - cuts[b])]
            sum_copies.append(send(block, block, ss_sem.at[k, b], sr_sem.at[k, b], peers[k]))
    for copy in sum_copies:
        copy.wait_recv()
    whole = parts[0]
    for k in range(1, n_layer):
        whole = whole + parts[k]
    out[0] = whole[:, :, :half]
    out[1] = whole[:, :, half:]

    for copy in edge_copies + mid_copies + col_copies + sum_copies:
        copy.wait_send()


def in_hbm(x):
    return pltpu.with_memory_space_constraint(x, pltpu.HBM)


def on_device(sizes, layers, wind, offsets, weights, sub_index):
    rows, cols = sub_index.shape
    tiles = cols // LANES
    groups = rows // SUB
    wide = groups + 2 * FOOT // SUB
    smem = pl.BlockSpec(memory_space=pltpu.SMEM)
    hbm = pl.BlockSpec(memory_space=pltpu.HBM)
    return pl.pallas_call(
        functools.partial(kernel, sizes),
        out_shape=pltpu.VMEM((2, DIRS, groups, cols // SUB), jnp.float32),
        in_specs=[hbm, hbm, hbm, hbm, hbm],
        out_specs=pl.BlockSpec(memory_space=pltpu.VMEM),
        scratch_shapes=[
            pltpu.SMEM((1, 2), jnp.int32),
            pltpu.SMEM((1, 2, DIRS), jnp.int32),
            pltpu.SemaphoreType.DMA((2,)),
            pltpu.VMEM((tiles + 2, rows + 2 * RIM, LANES), jnp.float32),
            pltpu.VMEM((tiles + 2, SUB, wide, LANES), jnp.float32),
            pltpu.VMEM(weights.shape, weights.dtype),
            pltpu.VMEM((DIRS, 2, tiles, rows, LANES), jnp.float32),
            pltpu.VMEM(sub_index.shape, sub_index.dtype),
            pltpu.VMEM((sizes[0], DIRS, groups, LANES), jnp.float32),
            pltpu.SemaphoreType.DMA((tiles + 2,)),
            pltpu.SemaphoreType.DMA((tiles, 2)),
            pltpu.SemaphoreType.DMA((tiles, 2)),
            pltpu.SemaphoreType.DMA((2, 3)),
            pltpu.SemaphoreType.DMA((2, 3)),
            pltpu.SemaphoreType.DMA((sizes[0] - 1, 3)),
            pltpu.SemaphoreType.DMA((sizes[0] - 1, 3)),
        ],
        compiler_params=pltpu.CompilerParams(
            collective_id=0, has_side_effects=True, vmem_limit_bytes=32 * 1024 * 1024
        ),
    )(in_hbm(wind), in_hbm(jnp.swapaxes(offsets, 1, 2)), in_hbm(layers), in_hbm(weights), in_hbm(sub_index))


def solution(mesh):
    sizes = (mesh.shape["layer"], mesh.shape["tx"], mesh.shape["ty"])
    placed = (
        P("layer", "tx", "ty"),
        P("layer", None),
        P("layer", None, None),
        P(None, None, "tx", "ty"),
        P("tx", "ty"),
    )
    return jax.shard_map(
        functools.partial(on_device, sizes),
        mesh=mesh, in_specs=placed, out_specs=P(None, None, "tx", "ty"), check_vma=False,
    )
```

```python
import functools

import jax
import jax.numpy as jnp
from jax import lax
from jax.experimental import pallas as pl
from jax.experimental.pallas import tpu as pltpu
from jax.sharding import PartitionSpec as P

DIRS = 9
SUB = 8
LANES = 128
PAD = 72
MESH = pl.DeviceIdType.MESH
CUTS = (0, 3, 6, DIRS)
SPARE = 6


def kernel(
    sizes, wind_in, offsets_in, layers, weights, sub_index, out, wind, offsets, raw, wraw, sub, field, mixed,
    shifted, live, wlive, totals, parts, local_sem, zs_sem, zr_sem, xs_sem, xr_sem, cs_sem, cr_sem, ss_sem, sr_sem,
):
    n_layer, n_tx, n_ty = sizes
    rows, cols = sub_index.shape
    tiles = cols // LANES
    groups = rows // SUB
    wide = cols // SUB
    span = shifted.shape[1] // SUB
    layer = lax.axis_index("layer")
    tx = lax.axis_index("tx")
    ty = lax.axis_index("ty")
    up = {"tx": lax.rem(tx + n_tx - 1, n_tx)}
    down = {"tx": lax.rem(tx + 1, n_tx)}
    left = {"ty": lax.rem(ty + n_ty - 1, n_ty)}
    right = {"ty": lax.rem(ty + 1, n_ty)}
    peers = [{"layer": lax.rem(layer + k, n_layer)} for k in range(1, n_layer)]
    row_peers = [(down, 1)] if n_tx == 2 else [(down, 1), (up, 2)]
    col_peers = [(right, cols, 0), (left, PAD, PAD + cols)]

    order = [0, tiles - 1] + list(range(1, tiles - 1))
    own = {}
    for c in order:
        own[c] = pltpu.make_async_copy(layers.at[0, :, pl.ds(c * LANES, LANES)], raw.at[c], local_sem.at[c])
        own[c].start()
    local = [
        pltpu.make_async_copy(wind_in, wind, local_sem.at[tiles]),
        pltpu.make_async_copy(offsets_in, offsets, local_sem.at[tiles + 1]),
        pltpu.make_async_copy(sub_index, sub, local_sem.at[tiles + 2]),
        pltpu.make_async_copy(weights, wraw, local_sem.at[tiles + 3]),
    ]
    for copy in local:
        copy.start()

    barrier = pltpu.get_barrier_semaphore()
    greeted = [device for device, _ in row_peers] + [device for device, _, _ in col_peers] + peers
    greeted += [{**a, **b} for a, _ in row_peers for b, _, _ in col_peers]
    for device in greeted:
        pl.semaphore_signal(barrier, inc=1, device_id=device, device_id_type=MESH)

    for c in order:
        own[c].wait()
        field[0, pl.ds(PAD + c * LANES, LANES), :] = raw[c].T
    pl.semaphore_wait(barrier, len(greeted))

    def send(src, dst, send_sem, recv_sem, device):
        copy = pltpu.make_async_remote_copy(
            src_ref=src, dst_ref=dst, send_sem=send_sem, recv_sem=recv_sem,
            device_id=device, device_id_type=MESH,
        )
        copy.start()
        return copy

    side_copies, corner_copies = [], []
    for k, (b, start, end) in enumerate(col_peers):
        side_copies.append(send(
            field.at[0, pl.ds(start, PAD), :], field.at[0, pl.ds(end, PAD), :], zs_sem.at[k], zr_sem.at[k], b,
        ))
    for j, (a, slot) in enumerate(row_peers):
        for k, (b, start, end) in enumerate(col_peers):
            corner_copies.append(send(
                field.at[0, pl.ds(start, PAD), :], field.at[slot, pl.ds(end, PAD), :],
                cs_sem.at[j, k], cr_sem.at[j, k], {**a, **b},
            ))
    row_copies = [[
        send(
            field.at[0, pl.ds(PAD + c * LANES, LANES), :], field.at[slot, pl.ds(PAD + c * LANES, LANES), :],
            xs_sem.at[j, c], xr_sem.at[j, c], a,
        ) for j, (a, slot) in enumerate(row_peers)
    ] for c in range(tiles)]

    for copy in local:
        copy.wait()
    qrow = lax.shift_right_arithmetic(wind[0, 0], 6)
    qcol = lax.shift_right_arithmetic(wind[0, 1], 6)
    frow = (wind[0, 0] - 64 * qrow).astype(jnp.float32) / 64.0
    fcol = (wind[0, 1] - 64 * qcol).astype(jnp.float32) / 64.0

    for c in range(tiles):
        live[pl.ds(c * LANES, LANES), :] = (sub[:, pl.ds(c * LANES, LANES)] >= 0).astype(jnp.float32).T

    def prepare(d, carry):
        turn = (offsets[0, 0, d] - qrow) & (LANES - 1)
        for s in range(2):
            for c in range(tiles):
                w = wraw[d, s, :, pl.ds(c * LANES, LANES)].astype(jnp.float32).T
                w = pltpu.roll(w * live[pl.ds(c * LANES, LANES), :], turn, 1)
                for g in range(LANES // SUB):
                    wlive[d, s, pl.ds(c * (LANES // SUB) + g, SUB, stride=wide), :] = w[g * SUB : (g + 1) * SUB]
        return carry

    lax.fori_loop(0, DIRS, prepare, 0)

    def mix(start, size):
        lane = lax.broadcasted_iota(jnp.int32, (size, LANES), 1)
        here = [field[t, pl.ds(start, size), :] for t in range(len(row_peers) + 1)]
        turned = [pltpu.roll(h, 1, 1) for h in here]
        if n_tx == 2:
            before = [jnp.where(lane == 0, turned[1], turned[0]), jnp.where(lane == 0, turned[0], turned[1])]
        else:
            before = [
                jnp.where(lane == 0, turned[1], turned[0]), turned[1], jnp.where(lane == 0, turned[0], turned[2]),
            ]
        for t, (h, b) in enumerate(zip(here, before)):
            mixed[t, pl.ds(SUB + start, size), :] = (1.0 - frow) * h + frow * b
        for t in range(len(here)):
            for g in range(size // SUB):
                one = mixed[t, pl.ds(SUB + start + g * SUB, SUB), :]
                two = mixed[t, pl.ds(SUB - 1 + start + g * SUB, SUB), :]
                shifted[t, pl.ds(start // SUB + g, SUB, stride=span), :] = (1.0 - fcol) * one + fcol * two

    for t in range(len(row_peers) + 1):
        mixed[t, pl.ds(0, SUB), :] = jnp.zeros((SUB, LANES), jnp.float32)
    for copy in side_copies + corner_copies:
        copy.wait_recv()
    mix(0, PAD)
    for c in range(tiles):
        for copy in row_copies[c]:
            copy.wait_recv()
        mix(PAD + c * LANES, LANES)
    mix(PAD + cols, PAD)

    lane_w = lax.broadcasted_iota(jnp.int32, (wide, LANES), 1)
    pick_row = lax.broadcasted_iota(jnp.int32, (groups, 2 * LANES), 0)
    pick_col = lax.broadcasted_iota(jnp.int32, (groups, 2 * LANES), 1)

    def slopes(d, carry):
        turn = offsets[0, 0, d] - qrow
        top = offsets[0, 1, d] - qcol + PAD
        inside = (lane_w >= turn) & (lane_w < LANES + turn)
        sums = [None, None]
        for r in range(SUB):
            start = ((top + r) & (SUB - 1)) * span + lax.shift_right_arithmetic(top + r, 3)
            seen = [shifted[t, pl.ds(start, wide), :] for t in range(len(row_peers) + 1)]
            other = seen[1] if n_tx == 2 else jnp.where(lane_w < turn, seen[2], seen[1])
            view = jnp.where(inside, seen[0], other)
            for s in range(2):
                term = wlive[d, s, pl.ds(r * wide, wide), :] * view
                sums[s] = term if r == 0 else sums[s] + term
        for s in range(2):
            high = sums[s].astype(jnp.bfloat16)
            totals[d, pl.ds(s * wide, wide), pl.ds(0, LANES)] = high
            totals[d, pl.ds(s * wide, wide), pl.ds(LANES, LANES)] = (
                sums[s] - high.astype(jnp.float32)
            ).astype(jnp.bfloat16)
        return carry

    def gather(d, carry):
        turn = offsets[0, 0, d] - qrow
        pick = (lax.shift_right_logical((pick_col - turn) & (LANES - 1), 3) == pick_row).astype(jnp.bfloat16)
        parts[layer, d, :, :] = lax.dot_general(
            pick, totals[d], (((1,), (1,)), ((), ())), preferred_element_type=jnp.float32
        )
        return carry

    sum_copies = []
    for b in range(len(CUTS) - 1):
        lax.fori_loop(CUTS[b], CUTS[b + 1], slopes, 0)
        for d in range(CUTS[b], CUTS[b + 1]):
            gather(d, 0)
        for k in range(n_layer - 1):
            block = parts.at[layer, pl.ds(CUTS[b], CUTS[b + 1] - CUTS[b])]
            sum_copies.append(send(block, block, ss_sem.at[k, b], sr_sem.at[k, b], peers[k]))
    for copy in sum_copies:
        copy.wait_recv()
    whole = parts[0]
    for k in range(1, n_layer):
        whole = whole + parts[k]
    out[0] = whole[:, :, :wide]
    out[1] = whole[:, :, wide:]

    for copy in side_copies + corner_copies + sum(row_copies, []) + sum_copies:
        copy.wait_send()


def in_hbm(x):
    return pltpu.with_memory_space_constraint(x, pltpu.HBM)


def on_device(sizes, layers, wind, offsets, weights, sub_index):
    rows, cols = sub_index.shape
    tiles = cols // LANES
    groups = rows // SUB
    wide = cols // SUB
    seen = 2 if sizes[1] == 2 else 3
    deep = cols + 2 * PAD
    hbm = pl.BlockSpec(memory_space=pltpu.HBM)
    dma = pltpu.SemaphoreType.DMA
    return pl.pallas_call(
        functools.partial(kernel, sizes),
        out_shape=pltpu.VMEM((2, DIRS, groups, wide), jnp.float32),
        in_specs=[hbm] * 5,
        out_specs=pl.BlockSpec(memory_space=pltpu.VMEM),
        scratch_shapes=[
            pltpu.SMEM((1, 2), jnp.int32),
            pltpu.SMEM((1, 2, DIRS), jnp.int32),
            pltpu.VMEM((tiles, rows, LANES), jnp.float32),
            pltpu.VMEM(weights.shape, weights.dtype),
            pltpu.VMEM(sub_index.shape, sub_index.dtype),
            pltpu.VMEM((seen, deep, LANES), jnp.float32),
            pltpu.VMEM((seen, deep + SUB, LANES), jnp.float32),
            pltpu.VMEM((seen, deep + SPARE * SUB, LANES), jnp.float32),
            pltpu.VMEM((cols, LANES), jnp.float32),
            pltpu.VMEM((DIRS, 2, cols, LANES), jnp.float32),
            pltpu.VMEM((DIRS, 2 * wide, 2 * LANES), jnp.bfloat16),
            pltpu.VMEM((sizes[0], DIRS, groups, LANES), jnp.float32),
            dma((tiles + 4,)),
            dma((2,)),
            dma((2,)),
            dma((seen - 1, tiles)),
            dma((seen - 1, tiles)),
            dma((seen - 1, 2)),
            dma((seen - 1, 2)),
            dma((sizes[0] - 1, len(CUTS) - 1)),
            dma((sizes[0] - 1, len(CUTS) - 1)),
        ],
        compiler_params=pltpu.CompilerParams(
            collective_id=0, has_side_effects=True, vmem_limit_bytes=32 * 1024 * 1024
        ),
    )(in_hbm(wind), in_hbm(jnp.swapaxes(offsets, 1, 2)), in_hbm(layers), in_hbm(weights), in_hbm(sub_index))


def solution(mesh):
    sizes = (mesh.shape["layer"], mesh.shape["tx"], mesh.shape["ty"])
    placed = (
        P("layer", "tx", "ty"),
        P("layer", None),
        P("layer", None, None),
        P(None, None, "tx", "ty"),
        P("tx", "ty"),
    )
    return jax.shard_map(
        functools.partial(on_device, sizes),
        mesh=mesh, in_specs=placed, out_specs=P(None, None, "tx", "ty"), check_vma=False,
    )
```

```python
import functools

import jax
import jax.numpy as jnp
from jax import lax
from jax.experimental import pallas as pl
from jax.experimental.pallas import tpu as pltpu
from jax.sharding import PartitionSpec as P

DIRS = 9
SUB = 8
LANES = 128
PAD = 72
MESH = pl.DeviceIdType.MESH
SPARE = 6


def kernel(
    sizes, wind_in, offsets_in, layers, weights, sub_index, out, wind, offsets, raw, wraw, sub, field, mixed,
    shifted, live, wlive, totals, parts, local_sem, zs_sem, zr_sem, xs_sem, xr_sem, cs_sem, cr_sem, ss_sem, sr_sem,
):
    n_layer, n_tx, n_ty = sizes
    rows, cols = sub_index.shape
    tiles = cols // LANES
    groups = rows // SUB
    wide = cols // SUB
    span = shifted.shape[1] // SUB
    layer = lax.axis_index("layer")
    tx = lax.axis_index("tx")
    ty = lax.axis_index("ty")
    up = {"tx": lax.rem(tx + n_tx - 1, n_tx)}
    down = {"tx": lax.rem(tx + 1, n_tx)}
    left = {"ty": lax.rem(ty + n_ty - 1, n_ty)}
    right = {"ty": lax.rem(ty + 1, n_ty)}
    peers = [{"layer": lax.rem(layer + k, n_layer)} for k in range(1, n_layer)]
    row_peers = [(down, 1)] if n_tx == 2 else [(down, 1), (up, 2)]
    col_peers = [(right, cols, 0), (left, PAD, PAD + cols)]
    ends = [PAD + min((c + 1) * LANES + PAD, cols) for c in range(tiles)]
    chunks = list(zip([PAD] + ends[:-1], ends))

    order = [0, tiles - 1] + list(range(1, tiles - 1))
    own = {}
    for c in order:
        own[c] = pltpu.make_async_copy(layers.at[0, :, pl.ds(c * LANES, LANES)], raw.at[c], local_sem.at[c])
        own[c].start()
    local = [
        pltpu.make_async_copy(wind_in, wind, local_sem.at[tiles]),
        pltpu.make_async_copy(offsets_in, offsets, local_sem.at[tiles + 1]),
        pltpu.make_async_copy(sub_index, sub, local_sem.at[tiles + 2]),
        pltpu.make_async_copy(weights, wraw, local_sem.at[tiles + 3]),
    ]
    for copy in local:
        copy.start()

    barrier = pltpu.get_barrier_semaphore()
    greeted = [device for device, _ in row_peers] + [device for device, _, _ in col_peers] + peers
    greeted += [{**a, **b} for a, _ in row_peers for b, _, _ in col_peers]
    for device in greeted:
        pl.semaphore_signal(barrier, inc=1, device_id=device, device_id_type=MESH)

    for c in order:
        own[c].wait()
        field[0, pl.ds(PAD + c * LANES, LANES), :] = raw[c].T
    pl.semaphore_wait(barrier, len(greeted))

    def send(src, dst, send_sem, recv_sem, device):
        copy = pltpu.make_async_remote_copy(
            src_ref=src, dst_ref=dst, send_sem=send_sem, recv_sem=recv_sem,
            device_id=device, device_id_type=MESH,
        )
        copy.start()
        return copy

    side_copies, corner_copies = [], []
    for k, (b, start, end) in enumerate(col_peers):
        side_copies.append(send(
            field.at[0, pl.ds(start, PAD), :], field.at[0, pl.ds(end, PAD), :], zs_sem.at[k], zr_sem.at[k], b,
        ))
    for j, (a, slot) in enumerate(row_peers):
        for k, (b, start, end) in enumerate(col_peers):
            corner_copies.append(send(
                field.at[0, pl.ds(start, PAD), :], field.at[slot, pl.ds(end, PAD), :],
                cs_sem.at[j, k], cr_sem.at[j, k], {**a, **b},
            ))
    row_copies = [[
        send(
            field.at[0, pl.ds(start, end - start), :], field.at[slot, pl.ds(start, end - start), :],
            xs_sem.at[j, c], xr_sem.at[j, c], a,
        ) for j, (a, slot) in enumerate(row_peers)
    ] for c, (start, end) in enumerate(chunks)]

    for copy in local:
        copy.wait()
    qrow = lax.shift_right_arithmetic(wind[0, 0], 6)
    qcol = lax.shift_right_arithmetic(wind[0, 1], 6)
    frow = (wind[0, 0] - 64 * qrow).astype(jnp.float32) / 64.0
    fcol = (wind[0, 1] - 64 * qcol).astype(jnp.float32) / 64.0

    for c in range(tiles):
        live[pl.ds(c * LANES, LANES), :] = (sub[:, pl.ds(c * LANES, LANES)] >= 0).astype(jnp.float32).T

    def prepare(d, carry):
        turn = (offsets[0, 0, d] - qrow) & (LANES - 1)
        for s in range(2):
            for c in range(tiles):
                w = wraw[d, s, :, pl.ds(c * LANES, LANES)].astype(jnp.float32).T
                w = pltpu.roll(w * live[pl.ds(c * LANES, LANES), :], turn, 1)
                for g in range(LANES // SUB):
                    wlive[d, s, pl.ds(c * (LANES // SUB) + g, SUB, stride=wide), :] = w[g * SUB : (g + 1) * SUB]
        return carry

    lax.fori_loop(0, DIRS, prepare, 0)

    def mix(start, size):
        for at in range(start, start + size, SUB):
            mix_group(at)

    def mix_group(start):
        size = SUB
        lane = lax.broadcasted_iota(jnp.int32, (size, LANES), 1)
        here = [field[t, pl.ds(start, size), :] for t in range(len(row_peers) + 1)]
        turned = [pltpu.roll(h, 1, 1) for h in here]
        if n_tx == 2:
            before = [jnp.where(lane == 0, turned[1], turned[0]), jnp.where(lane == 0, turned[0], turned[1])]
        else:
            before = [
                jnp.where(lane == 0, turned[1], turned[0]), turned[1], jnp.where(lane == 0, turned[0], turned[2]),
            ]
        for t, (h, b) in enumerate(zip(here, before)):
            mixed[t, pl.ds(SUB + start, size), :] = (1.0 - frow) * h + frow * b
        for t in range(len(here)):
            for g in range(size // SUB):
                one = mixed[t, pl.ds(SUB + start + g * SUB, SUB), :]
                two = mixed[t, pl.ds(SUB - 1 + start + g * SUB, SUB), :]
                shifted[t, pl.ds(start // SUB + g, SUB, stride=span), :] = (1.0 - fcol) * one + fcol * two

    part = LANES // SUB
    lane_w = lax.broadcasted_iota(jnp.int32, (part, LANES), 1)
    pick_row = lax.broadcasted_iota(jnp.int32, (groups, 2 * LANES), 0)
    pick_col = lax.broadcasted_iota(jnp.int32, (groups, 2 * LANES), 1)
    pick = (lax.shift_right_logical(pick_col & (LANES - 1), 3) == pick_row).astype(jnp.bfloat16)

    def slopes(c, d):
        turn = offsets[0, 0, d] - qrow
        top = offsets[0, 1, d] - qcol + PAD
        inside = (lane_w >= turn) & (lane_w < LANES + turn)
        sums = [None, None]
        for r in range(SUB):
            start = ((top + r) & (SUB - 1)) * span + lax.shift_right_arithmetic(top + r, 3) + c * part
            seen = [shifted[t, pl.ds(start, part), :] for t in range(len(row_peers) + 1)]
            other = seen[1] if n_tx == 2 else jnp.where(lane_w < turn, seen[2], seen[1])
            view = jnp.where(inside, seen[0], other)
            for s in range(2):
                term = wlive[d, s, pl.ds(r * wide + c * part, part), :] * view
                sums[s] = term if r == 0 else sums[s] + term
        for s in range(2):
            item = 2 * d + s
            place = (item & ~(SUB - 1)) + ((item + c) & (SUB - 1))
            back = pltpu.roll(sums[s], (-turn) & (LANES - 1), 1)
            high = back.astype(jnp.bfloat16)
            low = (back - high.astype(jnp.float32)).astype(jnp.bfloat16)
            at = pl.ds(pl.multiple_of(place * part, part), part)
            totals[c, at, pl.ds(0, LANES)] = high
            totals[c, at, pl.ds(LANES, LANES)] = low

    def three(c, i, carry):
        for k in range(3):
            slopes(c, 3 * i + k)
        return carry

    totals[...] = jnp.zeros_like(totals)
    for t in range(len(row_peers) + 1):
        mixed[t, pl.ds(0, SUB), :] = jnp.zeros((SUB, LANES), jnp.float32)
    sum_copies = []
    for c in range(tiles):
        if c == 0:
            for copy in side_copies + corner_copies:
                copy.wait_recv()
            mix(0, PAD)
        for copy in row_copies[c]:
            copy.wait_recv()
        mix(chunks[c][0], chunks[c][1] - chunks[c][0])
        if c == tiles - 1:
            mix(PAD + cols, PAD)
        lax.fori_loop(0, DIRS // 3, functools.partial(three, c), 0)
        parts[layer, c, :, :] = lax.dot_general(
            pick, totals[c], (((1,), (1,)), ((), ())), preferred_element_type=jnp.float32
        )
        block = parts.at[layer, c]
        sum_copies.append([
            send(block, block, ss_sem.at[k, c], sr_sem.at[k, c], peers[k]) for k in range(n_layer - 1)
        ])
    whole = []
    for c in range(tiles):
        for copy in sum_copies[c]:
            copy.wait_recv()
        total = parts[0, c]
        for k in range(1, n_layer):
            total = total + parts[k, c]
        whole.append(total)
    lane_g = lax.broadcasted_iota(jnp.int32, (groups, LANES), 1)
    for d in range(DIRS):
        for s in range(2):
            item = 2 * d + s
            first = item & (SUB - 1)
            block = None
            for c in range(tiles):
                slot = (first + c) & (SUB - 1)
                piece = whole[c][:, item // SUB * LANES : (item // SUB + 1) * LANES]
                inside = (lane_g >= slot * part) & (lane_g < (slot + 1) * part)
                block = piece if block is None else jnp.where(inside, piece, block)
            if first:
                block = pltpu.roll(block, LANES - first * part, 1)
            out[s, d] = block[:, :wide]

    for copy in side_copies + corner_copies + sum(row_copies, []) + sum(sum_copies, []):
        copy.wait_send()


def in_hbm(x):
    return pltpu.with_memory_space_constraint(x, pltpu.HBM)


def on_device(sizes, layers, wind, offsets, weights, sub_index):
    rows, cols = sub_index.shape
    tiles = cols // LANES
    groups = rows // SUB
    wide = cols // SUB
    seen = 2 if sizes[1] == 2 else 3
    deep = cols + 2 * PAD
    deep_out = -(-2 * DIRS // SUB) * LANES
    hbm = pl.BlockSpec(memory_space=pltpu.HBM)
    dma = pltpu.SemaphoreType.DMA
    return pl.pallas_call(
        functools.partial(kernel, sizes),
        out_shape=pltpu.VMEM((2, DIRS, groups, wide), jnp.float32),
        in_specs=[hbm] * 5,
        out_specs=pl.BlockSpec(memory_space=pltpu.VMEM),
        scratch_shapes=[
            pltpu.SMEM((1, 2), jnp.int32),
            pltpu.SMEM((1, 2, DIRS), jnp.int32),
            pltpu.VMEM((tiles, rows, LANES), jnp.float32),
            pltpu.VMEM(weights.shape, weights.dtype),
            pltpu.VMEM(sub_index.shape, sub_index.dtype),
            pltpu.VMEM((seen, deep, LANES), jnp.float32),
            pltpu.VMEM((seen, deep + SUB, LANES), jnp.float32),
            pltpu.VMEM((seen, deep + SPARE * SUB, LANES), jnp.float32),
            pltpu.VMEM((cols, LANES), jnp.float32),
            pltpu.VMEM((DIRS, 2, cols, LANES), jnp.float32),
            pltpu.VMEM((tiles, deep_out, 2 * LANES), jnp.bfloat16),
            pltpu.VMEM((sizes[0], tiles, groups, deep_out), jnp.float32),
            dma((tiles + 4,)),
            dma((2,)),
            dma((2,)),
            dma((seen - 1, tiles)),
            dma((seen - 1, tiles)),
            dma((seen - 1, 2)),
            dma((seen - 1, 2)),
            dma((sizes[0] - 1, tiles)),
            dma((sizes[0] - 1, tiles)),
        ],
        compiler_params=pltpu.CompilerParams(
            collective_id=0, has_side_effects=True, vmem_limit_bytes=32 * 1024 * 1024
        ),
    )(in_hbm(wind), in_hbm(jnp.swapaxes(offsets, 1, 2)), in_hbm(layers), in_hbm(weights), in_hbm(sub_index))


def solution(mesh):
    sizes = (mesh.shape["layer"], mesh.shape["tx"], mesh.shape["ty"])
    placed = (
        P("layer", "tx", "ty"),
        P("layer", None),
        P("layer", None, None),
        P(None, None, "tx", "ty"),
        P("tx", "ty"),
    )
    return jax.shard_map(
        functools.partial(on_device, sizes),
        mesh=mesh, in_specs=placed, out_specs=P(None, None, "tx", "ty"), check_vma=False,
    )
```

```python
import functools

import jax
import jax.numpy as jnp
from jax import lax
from jax.experimental import pallas as pl
from jax.experimental.pallas import tpu as pltpu
from jax.sharding import PartitionSpec as P

DIRS = 9
SUB = 8
LANES = 128
PAD = 72
MESH = pl.DeviceIdType.MESH
SPARE = 6


def kernel(
    sizes, wind_in, offsets_in, layers, weights, sub_index, out, wind, offsets, raw, wraw, sub, field, mixed,
    shifted, live, wlive, totals, parts, local_sem, zs_sem, zr_sem, xs_sem, xr_sem, cs_sem, cr_sem, ss_sem, sr_sem, ready,
):
    n_layer, n_tx, n_ty = sizes
    rows, cols = sub_index.shape
    tiles = cols // LANES
    groups = rows // SUB
    wide = cols // SUB
    span = shifted.shape[1] // SUB
    layer = lax.axis_index("layer")
    tx = lax.axis_index("tx")
    ty = lax.axis_index("ty")
    up = {"tx": lax.rem(tx + n_tx - 1, n_tx)}
    down = {"tx": lax.rem(tx + 1, n_tx)}
    left = {"ty": lax.rem(ty + n_ty - 1, n_ty)}
    right = {"ty": lax.rem(ty + 1, n_ty)}
    peers = [{"layer": lax.rem(layer + k, n_layer)} for k in range(1, n_layer)]
    row_peers = [(down, 1)] if n_tx == 2 else [(down, 1), (up, 2)]
    col_peers = [(right, cols, 0), (left, PAD, PAD + cols)]
    stages = list(range(1, tiles - 1)) + [0, tiles - 1]
    cut = [PAD + LANES - PAD] + [PAD + (c + 1) * LANES + PAD for c in range(1, tiles - 1)]
    chunks = list(zip(cut[:-1], cut[1:])) + [(PAD, cut[0]), (cut[-1], PAD + cols)]

    order = [0, tiles - 1] + list(range(1, tiles - 1))
    own = {}
    for c in order:
        own[c] = pltpu.make_async_copy(layers.at[0, :, pl.ds(c * LANES, LANES)], raw.at[c], local_sem.at[c])
        own[c].start()
    local = [
        pltpu.make_async_copy(wind_in, wind, local_sem.at[tiles]),
        pltpu.make_async_copy(offsets_in, offsets, local_sem.at[tiles + 1]),
        pltpu.make_async_copy(sub_index, sub, local_sem.at[tiles + 2]),
        pltpu.make_async_copy(weights, wraw, local_sem.at[tiles + 3]),
    ]
    for copy in local:
        copy.start()

    barrier = pltpu.get_barrier_semaphore()
    def signal(semaphore, devices):
        for device in devices:
            pl.semaphore_signal(semaphore, inc=1, device_id=device, device_id_type=MESH)

    at_right = [right] + [{**a, **right} for a, _ in row_peers]
    at_left = [left] + [{**a, **left} for a, _ in row_peers]
    same = [device for device, _ in row_peers] + peers
    ahead_right = ty != 0
    ahead_left = ty == 1
    signal(barrier, same)

    @pl.when(ty != 1)
    def _():
        signal(barrier, at_left)

    @pl.when(ty == 0)
    def _():
        signal(barrier, at_right)

    for c in order:
        own[c].wait()
        field[0, pl.ds(PAD + c * LANES, LANES), :] = raw[c].T
    pl.semaphore_wait(
        barrier,
        len(same) + len(at_right) * ahead_right.astype(jnp.int32) + len(at_left) * ahead_left.astype(jnp.int32),
    )

    def plan(src, dst, send_sem, recv_sem, device):
        return pltpu.make_async_remote_copy(
            src_ref=src, dst_ref=dst, send_sem=send_sem, recv_sem=recv_sem,
            device_id=device, device_id_type=MESH,
        )

    def send(*args):
        copy = plan(*args)
        copy.start()
        return copy

    col_copies = [[], []]
    for k, (b, start, end) in enumerate(col_peers):
        col_copies[k].append(plan(
            field.at[0, pl.ds(start, PAD), :], field.at[0, pl.ds(end, PAD), :], zs_sem.at[k], zr_sem.at[k], b,
        ))
        for j, (a, slot) in enumerate(row_peers):
            col_copies[k].append(plan(
                field.at[0, pl.ds(start, PAD), :], field.at[slot, pl.ds(end, PAD), :],
                cs_sem.at[j, k], cr_sem.at[j, k], {**a, **b},
            ))

    def start_all(copies):
        for copy in copies:
            copy.start()

    @pl.when(ahead_right)
    def _():
        signal(ready, at_right)
        start_all(col_copies[0])

    @pl.when(ahead_left)
    def _():
        signal(ready, at_left)
        start_all(col_copies[1])

    row_copies = [[
        send(
            field.at[0, pl.ds(start, end - start), :], field.at[slot, pl.ds(start, end - start), :],
            xs_sem.at[j, c], xr_sem.at[j, c], a,
        ) for j, (a, slot) in enumerate(row_peers)
    ] for c, (start, end) in enumerate(chunks)]

    for copy in local:
        copy.wait()
    qrow = lax.shift_right_arithmetic(wind[0, 0], 6)
    qcol = lax.shift_right_arithmetic(wind[0, 1], 6)
    frow = (wind[0, 0] - 64 * qrow).astype(jnp.float32) / 64.0
    fcol = (wind[0, 1] - 64 * qcol).astype(jnp.float32) / 64.0

    def prepare(c, i, carry):
        for k in range(3):
            d = 3 * i + k
            turn = (offsets[0, 0, d] - qrow) & (LANES - 1)
            for s in range(2):
                w = wraw[d, s, :, pl.ds(c * LANES, LANES)].T.astype(jnp.float32)
                w = pltpu.roll(w * live[pl.ds(c * LANES, LANES), :], turn, 1)
                for g in range(LANES // SUB):
                    wlive[d, s, pl.ds(c * (LANES // SUB) + g, SUB, stride=wide), :] = w[g * SUB : (g + 1) * SUB]
        return carry

    def prepare_all(c):
        live[pl.ds(c * LANES, LANES), :] = (sub[:, pl.ds(c * LANES, LANES)] >= 0).astype(jnp.float32).T
        lax.fori_loop(0, DIRS // 3, functools.partial(prepare, c), 0)

    for c in stages[:2]:
        prepare_all(c)

    @pl.when(ty != 1)
    def _():
        pl.semaphore_wait(ready, len(at_left) + len(at_right) * (ty == 0).astype(jnp.int32))
        start_all(col_copies[1])

    @pl.when(ty == 0)
    def _():
        start_all(col_copies[0])

    for c in stages[2:]:
        prepare_all(c)

    def mix(start, size):
        for at in range(start, start + size, SUB):
            mix_group(at)

    def mix_group(start):
        size = SUB
        lane = lax.broadcasted_iota(jnp.int32, (size, LANES), 1)
        here = [field[t, pl.ds(start, size), :] for t in range(len(row_peers) + 1)]
        turned = [pltpu.roll(h, 1, 1) for h in here]
        if n_tx == 2:
            before = [jnp.where(lane == 0, turned[1], turned[0]), jnp.where(lane == 0, turned[0], turned[1])]
        else:
            before = [
                jnp.where(lane == 0, turned[1], turned[0]), turned[1], jnp.where(lane == 0, turned[0], turned[2]),
            ]
        for t, (h, b) in enumerate(zip(here, before)):
            mixed[t, pl.ds(SUB + start, size), :] = (1.0 - frow) * h + frow * b
        for t in range(len(here)):
            for g in range(size // SUB):
                one = mixed[t, pl.ds(SUB + start + g * SUB, SUB), :]
                two = mixed[t, pl.ds(SUB - 1 + start + g * SUB, SUB), :]
                shifted[t, pl.ds(start // SUB + g, SUB, stride=span), :] = (1.0 - fcol) * one + fcol * two

    part = LANES // SUB
    lane_w = lax.broadcasted_iota(jnp.int32, (part, LANES), 1)
    pick_row = lax.broadcasted_iota(jnp.int32, (groups, 2 * LANES), 0)
    pick_col = lax.broadcasted_iota(jnp.int32, (groups, 2 * LANES), 1)
    pick = (lax.shift_right_logical(pick_col & (LANES - 1), 3) == pick_row).astype(jnp.bfloat16)

    def slopes(c, d):
        turn = offsets[0, 0, d] - qrow
        top = offsets[0, 1, d] - qcol + PAD
        inside = (lane_w >= turn) & (lane_w < LANES + turn)
        sums = [None, None]
        for r in range(SUB):
            start = ((top + r) & (SUB - 1)) * span + lax.shift_right_arithmetic(top + r, 3) + c * part
            seen = [shifted[t, pl.ds(start, part), :] for t in range(len(row_peers) + 1)]
            other = seen[1] if n_tx == 2 else jnp.where(lane_w < turn, seen[2], seen[1])
            view = jnp.where(inside, seen[0], other)
            for s in range(2):
                term = wlive[d, s, pl.ds(r * wide + c * part, part), :] * view
                sums[s] = term if r == 0 else sums[s] + term
        for s in range(2):
            item = 2 * d + s
            place = 2 * SUB * stages.index(c) + (item & SUB) + ((item + c) & (SUB - 1))
            place = jnp.where(d == DIRS - 1, 2 * SUB * tiles + s * tiles + c, place)
            back = pltpu.roll(sums[s], (-turn) & (LANES - 1), 1)
            high = back.astype(jnp.bfloat16)
            low = (back - high.astype(jnp.float32)).astype(jnp.bfloat16)
            at = pl.ds(pl.multiple_of(place * part, part), part)
            totals[at, pl.ds(0, LANES)] = high
            totals[at, pl.ds(LANES, LANES)] = low

    def three(c, i, carry):
        for k in range(3):
            slopes(c, 3 * i + k)
        return carry

    for t in range(len(row_peers) + 1):
        mixed[t, pl.ds(0, SUB), :] = jnp.zeros((SUB, LANES), jnp.float32)
    lines = [(2 * LANES * i, 2 * LANES) for i in range(tiles - 1)] + [(2 * LANES * (tiles - 1), 3 * LANES)]
    sum_copies = []
    for i, c in enumerate(stages):
        for copy in row_copies[i]:
            copy.wait_recv()
        if c == 0:
            for copy in col_copies[0]:
                copy.wait_recv()
            mix(0, PAD)
        mix(chunks[i][0], chunks[i][1] - chunks[i][0])
        if c == 0:
            mix(chunks[0][0], SUB)
        if c == tiles - 1:
            for copy in col_copies[1]:
                copy.wait_recv()
            mix(PAD + cols, PAD)
        lax.fori_loop(0, DIRS // 3, functools.partial(three, c), 0)
        line = pl.ds(*lines[i])
        parts[layer, :, line] = lax.dot_general(
            pick, totals[line, :], (((1,), (1,)), ((), ())), preferred_element_type=jnp.float32
        )
        block = parts.at[layer, :, line]
        sum_copies.append([
            send(block, block, ss_sem.at[k, i], sr_sem.at[k, i], peers[k]) for k in range(n_layer - 1)
        ])
    whole = {}
    for i, c in enumerate(stages):
        for copy in sum_copies[i]:
            copy.wait_recv()
        line = pl.ds(*lines[i])
        total = parts[0, :, line]
        for k in range(1, n_layer):
            total = total + parts[k, :, line]
        whole[c] = total
    lane_g = lax.broadcasted_iota(jnp.int32, (groups, LANES), 1)
    for d in range(DIRS - 1):
        for s in range(2):
            item = 2 * d + s
            first = item & (SUB - 1)
            block = None
            for c in range(tiles):
                slot = (first + c) & (SUB - 1)
                piece = whole[c][:, item // SUB * LANES : (item // SUB + 1) * LANES]
                inside = (lane_g >= slot * part) & (lane_g < (slot + 1) * part)
                block = piece if block is None else jnp.where(inside, piece, block)
            if first:
                block = pltpu.roll(block, LANES - first * part, 1)
            out[s, d] = block[:, :wide]
    block = whole[tiles - 1][:, 2 * LANES :]
    out[0, DIRS - 1] = block[:, :wide]
    out[1, DIRS - 1] = block[:, wide:]

    for copy in col_copies[0] + col_copies[1] + sum(row_copies, []) + sum(sum_copies, []):
        copy.wait_send()


def in_hbm(x):
    return pltpu.with_memory_space_constraint(x, pltpu.HBM)


def on_device(sizes, layers, wind, offsets, weights, sub_index):
    rows, cols = sub_index.shape
    tiles = cols // LANES
    groups = rows // SUB
    wide = cols // SUB
    seen = 2 if sizes[1] == 2 else 3
    deep = cols + 2 * PAD
    deep_out = (2 * tiles + 1) * LANES
    hbm = pl.BlockSpec(memory_space=pltpu.HBM)
    dma = pltpu.SemaphoreType.DMA
    return pl.pallas_call(
        functools.partial(kernel, sizes),
        out_shape=pltpu.VMEM((2, DIRS, groups, wide), jnp.float32),
        in_specs=[hbm] * 5,
        out_specs=pl.BlockSpec(memory_space=pltpu.VMEM),
        scratch_shapes=[
            pltpu.SMEM((1, 2), jnp.int32),
            pltpu.SMEM((1, 2, DIRS), jnp.int32),
            pltpu.VMEM((tiles, rows, LANES), jnp.float32),
            pltpu.VMEM(weights.shape, weights.dtype),
            pltpu.VMEM(sub_index.shape, sub_index.dtype),
            pltpu.VMEM((seen, deep, LANES), jnp.float32),
            pltpu.VMEM((seen, deep + SUB, LANES), jnp.float32),
            pltpu.VMEM((seen, deep + SPARE * SUB, LANES), jnp.float32),
            pltpu.VMEM((cols, LANES), jnp.float32),
            pltpu.VMEM((DIRS, 2, cols, LANES), jnp.float32),
            pltpu.VMEM((deep_out, 2 * LANES), jnp.bfloat16),
            pltpu.VMEM((sizes[0], groups, deep_out), jnp.float32),
            dma((tiles + 4,)),
            dma((2,)),
            dma((2,)),
            dma((seen - 1, tiles)),
            dma((seen - 1, tiles)),
            dma((seen - 1, 2)),
            dma((seen - 1, 2)),
            dma((sizes[0] - 1, tiles)),
            dma((sizes[0] - 1, tiles)),
            pltpu.SemaphoreType.REGULAR,
        ],
        compiler_params=pltpu.CompilerParams(
            collective_id=0, has_side_effects=True, vmem_limit_bytes=32 * 1024 * 1024
        ),
    )(in_hbm(wind), in_hbm(jnp.swapaxes(offsets, 1, 2)), in_hbm(layers), in_hbm(weights), in_hbm(sub_index))


def solution(mesh):
    sizes = (mesh.shape["layer"], mesh.shape["tx"], mesh.shape["ty"])
    placed = (
        P("layer", "tx", "ty"),
        P("layer", None),
        P("layer", None, None),
        P(None, None, "tx", "ty"),
        P("tx", "ty"),
    )
    return jax.shard_map(
        functools.partial(on_device, sizes),
        mesh=mesh, in_specs=placed, out_specs=P(None, None, "tx", "ty"), check_vma=False,
    )
```

```python
import functools

import jax
import jax.numpy as jnp
from jax import lax
from jax.experimental import pallas as pl
from jax.experimental.pallas import tpu as pltpu
from jax.sharding import PartitionSpec as P

DIRS = 9
SUB = 8
LANES = 128
PAD = 72
MESH = pl.DeviceIdType.MESH
SPARE = 6


def kernel(
    sizes, wind_in, offsets_in, layers, weights, sub_index, out, wind, offsets, raw, wraw, sub, field, mixed,
    shifted, live, wlive, totals, parts, local_sem, zs_sem, zr_sem, xs_sem, xr_sem, cs_sem, cr_sem, ss_sem, sr_sem, ready,
):
    n_layer, n_tx, n_ty = sizes
    rows, cols = sub_index.shape
    tiles = cols // LANES
    groups = rows // SUB
    wide = cols // SUB
    span = shifted.shape[1] // SUB
    layer = lax.axis_index("layer")
    tx = lax.axis_index("tx")
    ty = lax.axis_index("ty")
    up = {"tx": lax.rem(tx + n_tx - 1, n_tx)}
    down = {"tx": lax.rem(tx + 1, n_tx)}
    left = {"ty": lax.rem(ty + n_ty - 1, n_ty)}
    right = {"ty": lax.rem(ty + 1, n_ty)}
    peers = [{"layer": layer ^ k} for k in range(n_layer - 1, 0, -1)]
    row_peers = [(down, 1)] if n_tx == 2 else [(down, 1), (up, 2)]
    col_peers = [(right, cols, 0), (left, PAD, PAD + cols)]
    stages = [1, 0] + list(range(2, tiles))
    cut = [PAD, 2 * PAD] + [PAD + (c + 1) * LANES + PAD for c in range(1, tiles - 1)] + [PAD + cols]
    chunks = list(zip(cut[:-1], cut[1:]))

    order = [0, tiles - 1] + list(range(1, tiles - 1))
    own = {}
    for c in order:
        own[c] = pltpu.make_async_copy(layers.at[0, :, pl.ds(c * LANES, LANES)], raw.at[c], local_sem.at[c])
        own[c].start()
    local = [
        pltpu.make_async_copy(wind_in, wind, local_sem.at[tiles]),
        pltpu.make_async_copy(offsets_in, offsets, local_sem.at[tiles + 1]),
        pltpu.make_async_copy(sub_index, sub, local_sem.at[tiles + 2]),
        pltpu.make_async_copy(weights, wraw, local_sem.at[tiles + 3]),
    ]
    for copy in local:
        copy.start()

    barrier = pltpu.get_barrier_semaphore()
    def signal(semaphore, devices):
        for device in devices:
            pl.semaphore_signal(semaphore, inc=1, device_id=device, device_id_type=MESH)

    at_right = [right] + [{**a, **right} for a, _ in row_peers]
    at_left = [left] + [{**a, **left} for a, _ in row_peers]
    same = [device for device, _ in row_peers] + peers
    ahead_right = ty != 0
    ahead_left = ty == 1
    signal(barrier, same)

    @pl.when(ty != 1)
    def _():
        signal(barrier, at_left)

    @pl.when(ty == 0)
    def _():
        signal(barrier, at_right)

    for c in order:
        own[c].wait()
        field[0, pl.ds(PAD + c * LANES, LANES), :] = raw[c].T
    pl.semaphore_wait(
        barrier,
        len(same) + len(at_right) * ahead_right.astype(jnp.int32) + len(at_left) * ahead_left.astype(jnp.int32),
    )

    def plan(src, dst, send_sem, recv_sem, device):
        return pltpu.make_async_remote_copy(
            src_ref=src, dst_ref=dst, send_sem=send_sem, recv_sem=recv_sem,
            device_id=device, device_id_type=MESH,
        )

    def send(*args):
        copy = plan(*args)
        copy.start()
        return copy

    col_copies = [[], []]
    for k, (b, start, end) in enumerate(col_peers):
        col_copies[k].append(plan(
            field.at[0, pl.ds(start, PAD), :], field.at[0, pl.ds(end, PAD), :], zs_sem.at[k], zr_sem.at[k], b,
        ))
        for j, (a, slot) in enumerate(row_peers):
            col_copies[k].append(plan(
                field.at[k * slot, pl.ds(start, PAD), :], field.at[slot, pl.ds(end, PAD), :],
                cs_sem.at[j, k], cr_sem.at[j, k], b if k else {**a, **b},
            ))

    def start_all(copies):
        for copy in copies:
            copy.start()

    @pl.when(ahead_right)
    def _():
        signal(ready, [right])
        start_all(col_copies[0])

    @pl.when(ahead_left)
    def _():
        signal(ready, at_left)

    row_copies = [[
        send(
            field.at[0, pl.ds(start, end - start), :], field.at[slot, pl.ds(start, end - start), :],
            xs_sem.at[j, c], xr_sem.at[j, c], a,
        ) for j, (a, slot) in enumerate(row_peers)
    ] for c, (start, end) in enumerate(chunks)]

    for copy in local:
        copy.wait()
    qrow = lax.shift_right_arithmetic(wind[0, 0], 6)
    qcol = lax.shift_right_arithmetic(wind[0, 1], 6)
    frow = (wind[0, 0] - 64 * qrow).astype(jnp.float32) / 64.0
    fcol = (wind[0, 1] - 64 * qcol).astype(jnp.float32) / 64.0

    def prepare(c, i, carry):
        for k in range(3):
            d = 3 * i + k
            turn = (offsets[0, 0, d] - qrow) & (LANES - 1)
            for s in range(2):
                w = wraw[d, s, :, pl.ds(c * LANES, LANES)].T.astype(jnp.float32)
                w = pltpu.roll(w * live[pl.ds(c * LANES, LANES), :], turn, 1)
                for g in range(LANES // SUB):
                    wlive[d, s, pl.ds(c * (LANES // SUB) + g, SUB, stride=wide), :] = w[g * SUB : (g + 1) * SUB]
        return carry

    def prepare_all(c):
        live[pl.ds(c * LANES, LANES), :] = (sub[:, pl.ds(c * LANES, LANES)] >= 0).astype(jnp.float32).T
        lax.fori_loop(0, DIRS // 3, functools.partial(prepare, c), 0)

    for c in stages[:2]:
        prepare_all(c)

    @pl.when(ty != 1)
    def _():
        pl.semaphore_wait(ready, 1 + len(at_right) * (ty == 0).astype(jnp.int32))

    @pl.when(ty == 0)
    def _():
        start_all(col_copies[0])

    col_copies[1][0].start()
    for c in stages[2:]:
        prepare_all(c)
    for copy in row_copies[0]:
        copy.wait_recv()
    start_all(col_copies[1][1:])

    def mix(start, end):
        for at in range(start, end, SUB):
            mix_group(at)

    def mix_group(start):
        size = SUB
        lane = lax.broadcasted_iota(jnp.int32, (size, LANES), 1)
        here = [field[t, pl.ds(start, size), :] for t in range(len(row_peers) + 1)]
        turned = [pltpu.roll(h, 1, 1) for h in here]
        if n_tx == 2:
            before = [jnp.where(lane == 0, turned[1], turned[0]), jnp.where(lane == 0, turned[0], turned[1])]
        else:
            before = [
                jnp.where(lane == 0, turned[1], turned[0]), turned[1], jnp.where(lane == 0, turned[0], turned[2]),
            ]
        for t, (h, b) in enumerate(zip(here, before)):
            mixed[t, pl.ds(SUB + start, size), :] = (1.0 - frow) * h + frow * b
        for t in range(len(here)):
            for g in range(size // SUB):
                one = mixed[t, pl.ds(SUB + start + g * SUB, SUB), :]
                two = mixed[t, pl.ds(SUB - 1 + start + g * SUB, SUB), :]
                shifted[t, pl.ds(start // SUB + g, SUB, stride=span), :] = (1.0 - fcol) * one + fcol * two

    part = LANES // SUB
    lane_w = lax.broadcasted_iota(jnp.int32, (part, LANES), 1)
    pick_row = lax.broadcasted_iota(jnp.int32, (groups, 2 * LANES), 0)
    pick_col = lax.broadcasted_iota(jnp.int32, (groups, 2 * LANES), 1)
    pick = (lax.shift_right_logical(pick_col & (LANES - 1), 3) == pick_row).astype(jnp.bfloat16)

    def slopes(c, d):
        turn = offsets[0, 0, d] - qrow
        top = offsets[0, 1, d] - qcol + PAD
        inside = (lane_w >= turn) & (lane_w < LANES + turn)
        sums = [None, None]
        for r in range(SUB):
            start = ((top + r) & (SUB - 1)) * span + lax.shift_right_arithmetic(top + r, 3) + c * part
            seen = [shifted[t, pl.ds(start, part), :] for t in range(len(row_peers) + 1)]
            other = seen[1] if n_tx == 2 else jnp.where(lane_w < turn, seen[2], seen[1])
            view = jnp.where(inside, seen[0], other)
            for s in range(2):
                term = wlive[d, s, pl.ds(r * wide + c * part, part), :] * view
                sums[s] = term if r == 0 else sums[s] + term
        for s in range(2):
            item = 2 * d + s
            place = 2 * SUB * stages.index(c) + (item & SUB) + ((item + c) & (SUB - 1))
            if d == DIRS - 1:
                place = 2 * SUB * tiles + s * tiles + c
            back = pltpu.roll(sums[s], (-turn) & (LANES - 1), 1)
            high = back.astype(jnp.bfloat16)
            low = (back - high.astype(jnp.float32)).astype(jnp.bfloat16)
            at = pl.ds(place * part, part)
            totals[at, pl.ds(0, LANES)] = high
            totals[at, pl.ds(LANES, LANES)] = low

    def three(c, i, carry):
        for k in range(3):
            slopes(c, 3 * i + k)
        return carry

    for t in range(len(row_peers) + 1):
        mixed[t, pl.ds(0, SUB), :] = jnp.zeros((SUB, LANES), jnp.float32)
    lines = [(2 * LANES * i, 2 * LANES) for i in range(tiles - 1)] + [(2 * LANES * (tiles - 1), 3 * LANES)]
    sum_copies = []
    for i, c in enumerate(stages):
        if c:
            for copy in row_copies[c]:
                copy.wait_recv()
        if c == 1:
            mix(*chunks[0])
        if c == 0:
            for copy in col_copies[0]:
                copy.wait_recv()
            mix(0, PAD)
            mix(PAD, PAD + SUB)
        else:
            mix(*chunks[c])
        if c == tiles - 1:
            for copy in col_copies[1]:
                copy.wait_recv()
            mix(PAD + cols, 2 * PAD + cols)
        [slopes(c, d) for d in range(DIRS)]
        line = pl.ds(*lines[i])
        parts[layer, :, line] = lax.dot_general(
            pick, totals[line, :], (((1,), (1,)), ((), ())), preferred_element_type=jnp.float32
        )
        block = parts.at[layer, :, line]
        sum_copies.append([
            send(block, block, ss_sem.at[k, i], sr_sem.at[k, i], peers[k]) for k in range(n_layer - 1)
        ])
    whole = {}
    for i, c in enumerate(stages):
        for copy in sum_copies[i]:
            copy.wait_recv()
        line = pl.ds(*lines[i])
        total = parts[0, :, line]
        for k in range(1, n_layer):
            total = total + parts[k, :, line]
        whole[c] = total
    lane_g = lax.broadcasted_iota(jnp.int32, (groups, LANES), 1)
    for d in range(DIRS - 1):
        for s in range(2):
            item = 2 * d + s
            first = item & (SUB - 1)
            block = None
            for c in range(tiles):
                slot = (first + c) & (SUB - 1)
                piece = whole[c][:, item // SUB * LANES : (item // SUB + 1) * LANES]
                inside = (lane_g >= slot * part) & (lane_g < (slot + 1) * part)
                block = piece if block is None else jnp.where(inside, piece, block)
            if first:
                block = pltpu.roll(block, LANES - first * part, 1)
            out[s, d] = block[:, :wide]
    block = whole[tiles - 1][:, 2 * LANES :]
    out[0, DIRS - 1] = block[:, :wide]
    out[1, DIRS - 1] = block[:, wide:]

    for copy in col_copies[0] + col_copies[1] + sum(row_copies, []) + sum(sum_copies, []):
        copy.wait_send()


def in_hbm(x):
    return pltpu.with_memory_space_constraint(x, pltpu.HBM)


def on_device(sizes, layers, wind, offsets, weights, sub_index):
    rows, cols = sub_index.shape
    tiles = cols // LANES
    groups = rows // SUB
    wide = cols // SUB
    seen = 2 if sizes[1] == 2 else 3
    deep = cols + 2 * PAD
    deep_out = (2 * tiles + 1) * LANES
    hbm = pl.BlockSpec(memory_space=pltpu.HBM)
    dma = pltpu.SemaphoreType.DMA
    return pl.pallas_call(
        functools.partial(kernel, sizes),
        out_shape=pltpu.VMEM((2, DIRS, groups, wide), jnp.float32),
        in_specs=[hbm] * 5,
        out_specs=pl.BlockSpec(memory_space=pltpu.VMEM),
        scratch_shapes=[
            pltpu.SMEM((1, 2), jnp.int32),
            pltpu.SMEM((1, 2, DIRS), jnp.int32),
            pltpu.VMEM((tiles, rows, LANES), jnp.float32),
            pltpu.VMEM(weights.shape, weights.dtype),
            pltpu.VMEM(sub_index.shape, sub_index.dtype),
            pltpu.VMEM((seen, deep, LANES), jnp.float32),
            pltpu.VMEM((seen, deep + SUB, LANES), jnp.float32),
            pltpu.VMEM((seen, deep + SPARE * SUB, LANES), jnp.float32),
            pltpu.VMEM((cols, LANES), jnp.float32),
            pltpu.VMEM((DIRS, 2, cols, LANES), jnp.float32),
            pltpu.VMEM((deep_out, 2 * LANES), jnp.bfloat16),
            pltpu.VMEM((sizes[0], groups, deep_out), jnp.float32),
            dma((tiles + 4,)),
            dma((2,)),
            dma((2,)),
            dma((seen - 1, tiles)),
            dma((seen - 1, tiles)),
            dma((seen - 1, 2)),
            dma((seen - 1, 2)),
            dma((sizes[0] - 1, tiles)),
            dma((sizes[0] - 1, tiles)),
            pltpu.SemaphoreType.REGULAR,
        ],
        compiler_params=pltpu.CompilerParams(
            collective_id=0, has_side_effects=True, vmem_limit_bytes=32 * 1024 * 1024
        ),
    )(in_hbm(wind), in_hbm(jnp.swapaxes(offsets, 1, 2)), in_hbm(layers), in_hbm(weights), in_hbm(sub_index))


def solution(mesh):
    sizes = (mesh.shape["layer"], mesh.shape["tx"], mesh.shape["ty"])
    placed = (
        P("layer", "tx", "ty"),
        P("layer", None),
        P("layer", None, None),
        P(None, None, "tx", "ty"),
        P("tx", "ty"),
    )
    return jax.shard_map(
        functools.partial(on_device, sizes),
        mesh=mesh, in_specs=placed, out_specs=P(None, None, "tx", "ty"), check_vma=False,
    )
```

```python
import functools

import jax
import jax.numpy as jnp
from jax import lax
from jax.experimental import pallas as pl
from jax.experimental.pallas import tpu as pltpu
from jax.sharding import PartitionSpec as P

DIRS = 9
SUB = 8
LANES = 128
PAD = 72
MESH = pl.DeviceIdType.MESH
SPARE = 6


def kernel(
    sizes, wind_in, offsets_in, layers, weights, sub_index, out, wind, offsets, raw, wraw, sub, field, mixed,
    shifted, live, wlive, totals, parts, local_sem, zs_sem, zr_sem, xs_sem, xr_sem, cs_sem, cr_sem, ss_sem, sr_sem, ready,
):
    n_layer, n_tx, n_ty = sizes
    rows, cols = sub_index.shape
    tiles = cols // LANES
    groups = rows // SUB
    wide = cols // SUB
    span = shifted.shape[1] // SUB
    layer = lax.axis_index("layer")
    tx = lax.axis_index("tx")
    ty = lax.axis_index("ty")
    up = {"tx": lax.rem(tx + n_tx - 1, n_tx)}
    down = {"tx": lax.rem(tx + 1, n_tx)}
    left = {"ty": lax.rem(ty + n_ty - 1, n_ty)}
    right = {"ty": lax.rem(ty + 1, n_ty)}
    peers = [{"layer": layer ^ k} for k in range(n_layer - 1, 0, -1)]
    row_peers = [(down, 1)] if n_tx == 2 else [(down, 1), (up, 2)]
    col_peers = [(right, cols, 0), (left, PAD, PAD + cols)]
    stages = [1, 0] + list(range(2, tiles))
    cut = [PAD, 2 * PAD] + [PAD + (c + 1) * LANES + PAD for c in range(1, tiles - 1)] + [PAD + cols]
    chunks = list(zip(cut[:-1], cut[1:]))

    order = [0, tiles - 1] + list(range(1, tiles - 1))
    own = {}
    for c in order:
        own[c] = pltpu.make_async_copy(layers.at[0, :, pl.ds(c * LANES, LANES)], raw.at[c], local_sem.at[c])
        own[c].start()
    local = [
        pltpu.make_async_copy(wind_in, wind, local_sem.at[tiles]),
        pltpu.make_async_copy(offsets_in, offsets, local_sem.at[tiles + 1]),
        pltpu.make_async_copy(sub_index, sub, local_sem.at[tiles + 2]),
        pltpu.make_async_copy(weights, wraw, local_sem.at[tiles + 3]),
    ]
    for copy in local:
        copy.start()

    barrier = pltpu.get_barrier_semaphore()
    def signal(semaphore, devices):
        for device in devices:
            pl.semaphore_signal(semaphore, inc=1, device_id=device, device_id_type=MESH)

    at_right = [right] + [{**a, **right} for a, _ in row_peers]
    at_left = [left] + [{**a, **left} for a, _ in row_peers]
    same = [device for device, _ in row_peers] + peers
    ahead_right = ty != 0
    ahead_left = ty == 1
    signal(barrier, same)

    @pl.when(ty != 1)
    def _():
        signal(barrier, at_left)

    @pl.when(ty == 0)
    def _():
        signal(barrier, at_right)

    def turn_tile(c):
        own[c].wait()
        field[0, pl.ds(PAD + c * LANES, LANES), :] = raw[c].T

    turn_tile(0)
    pl.semaphore_wait(
        barrier,
        len(same) + len(at_right) * ahead_right.astype(jnp.int32) + len(at_left) * ahead_left.astype(jnp.int32),
    )

    def plan(src, dst, send_sem, recv_sem, device):
        return pltpu.make_async_remote_copy(
            src_ref=src, dst_ref=dst, send_sem=send_sem, recv_sem=recv_sem,
            device_id=device, device_id_type=MESH,
        )

    def send(*args):
        copy = plan(*args)
        copy.start()
        return copy

    col_copies = [[], []]
    for k, (b, start, end) in enumerate(col_peers):
        col_copies[k].append(plan(
            field.at[0, pl.ds(start, PAD), :], field.at[0, pl.ds(end, PAD), :], zs_sem.at[k], zr_sem.at[k], b,
        ))
        for j, (a, slot) in enumerate(row_peers):
            col_copies[k].append(plan(
                field.at[k * slot, pl.ds(start, PAD), :], field.at[slot, pl.ds(end, PAD), :],
                cs_sem.at[j, k], cr_sem.at[j, k], b if k else {**a, **b},
            ))

    def start_all(copies):
        for copy in copies:
            copy.start()

    def send_rows(c):
        start, end = chunks[c]
        return [
            send(
                field.at[0, pl.ds(start, end - start), :], field.at[slot, pl.ds(start, end - start), :],
                xs_sem.at[j, c], xr_sem.at[j, c], a,
            ) for j, (a, slot) in enumerate(row_peers)
        ]

    row_copies = [send_rows(0)]
    turn_tile(tiles - 1)

    @pl.when(ahead_right)
    def _():
        signal(ready, [right])
        start_all(col_copies[0])

    @pl.when(ahead_left)
    def _():
        signal(ready, at_left)

    for c in range(1, tiles):
        if c < tiles - 1:
            for t in range(1 if c == 1 else c + 1, c + 2):
                if t < tiles - 1:
                    turn_tile(t)
        row_copies.append(send_rows(c))

    for copy in local:
        copy.wait()
    qrow = lax.shift_right_arithmetic(wind[0, 0], 6)
    qcol = lax.shift_right_arithmetic(wind[0, 1], 6)
    frow = (wind[0, 0] - 64 * qrow).astype(jnp.float32) / 64.0
    fcol = (wind[0, 1] - 64 * qcol).astype(jnp.float32) / 64.0

    def prepare(c, i, carry):
        for k in range(3):
            d = 3 * i + k
            turn = (offsets[0, 0, d] - qrow) & (LANES - 1)
            for s in range(2):
                w = wraw[d, s, :, pl.ds(c * LANES, LANES)].T.astype(jnp.float32)
                w = pltpu.roll(w * live[pl.ds(c * LANES, LANES), :], turn, 1)
                for g in range(LANES // SUB):
                    wlive[d, s, pl.ds(c * (LANES // SUB) + g, SUB, stride=wide), :] = w[g * SUB : (g + 1) * SUB]
        return carry

    def prepare_all(c):
        live[pl.ds(c * LANES, LANES), :] = (sub[:, pl.ds(c * LANES, LANES)] >= 0).astype(jnp.float32).T
        lax.fori_loop(0, DIRS // 3, functools.partial(prepare, c), 0)

    for c in stages[:2]:
        prepare_all(c)

    @pl.when(ty != 1)
    def _():
        pl.semaphore_wait(ready, 1 + len(at_right) * (ty == 0).astype(jnp.int32))

    @pl.when(ty == 0)
    def _():
        start_all(col_copies[0])

    col_copies[1][0].start()
    for c in stages[2:-1]:
        prepare_all(c)
    for copy in row_copies[0]:
        copy.wait_recv()
    start_all(col_copies[1][1:])
    prepare_all(stages[-1])

    def mix(start, end):
        for at in range(start, end, SUB):
            mix_group(at)

    def mix_group(start):
        size = SUB
        lane = lax.broadcasted_iota(jnp.int32, (size, LANES), 1)
        here = [field[t, pl.ds(start, size), :] for t in range(len(row_peers) + 1)]
        turned = [pltpu.roll(h, 1, 1) for h in here]
        if n_tx == 2:
            before = [jnp.where(lane == 0, turned[1], turned[0]), jnp.where(lane == 0, turned[0], turned[1])]
        else:
            before = [
                jnp.where(lane == 0, turned[1], turned[0]), turned[1], jnp.where(lane == 0, turned[0], turned[2]),
            ]
        for t, (h, b) in enumerate(zip(here, before)):
            mixed[t, pl.ds(SUB + start, size), :] = (1.0 - frow) * h + frow * b
        for t in range(len(here)):
            for g in range(size // SUB):
                one = mixed[t, pl.ds(SUB + start + g * SUB, SUB), :]
                two = mixed[t, pl.ds(SUB - 1 + start + g * SUB, SUB), :]
                shifted[t, pl.ds(start // SUB + g, SUB, stride=span), :] = (1.0 - fcol) * one + fcol * two

    part = LANES // SUB
    lane_w = lax.broadcasted_iota(jnp.int32, (part, LANES), 1)
    pick_row = lax.broadcasted_iota(jnp.int32, (groups, 2 * LANES), 0)
    pick_col = lax.broadcasted_iota(jnp.int32, (groups, 2 * LANES), 1)
    pick = (lax.shift_right_logical(pick_col & (LANES - 1), 3) == pick_row).astype(jnp.bfloat16)

    def slopes(c, d):
        turn = offsets[0, 0, d] - qrow
        top = offsets[0, 1, d] - qcol + PAD
        inside = (lane_w >= turn) & (lane_w < LANES + turn)
        sums = [None, None]
        for r in range(SUB):
            start = ((top + r) & (SUB - 1)) * span + lax.shift_right_arithmetic(top + r, 3) + c * part
            seen = [shifted[t, pl.ds(start, part), :] for t in range(len(row_peers) + 1)]
            other = seen[1] if n_tx == 2 else jnp.where(lane_w < turn, seen[2], seen[1])
            view = jnp.where(inside, seen[0], other)
            for s in range(2):
                term = wlive[d, s, pl.ds(r * wide + c * part, part), :] * view
                sums[s] = term if r == 0 else sums[s] + term
        for s in range(2):
            item = 2 * d + s
            place = 2 * SUB * stages.index(c) + (item & SUB) + ((item + c) & (SUB - 1))
            if d == DIRS - 1:
                place = 2 * SUB * tiles + s * tiles + c
            back = pltpu.roll(sums[s], (-turn) & (LANES - 1), 1)
            high = back.astype(jnp.bfloat16)
            low = (back - high.astype(jnp.float32)).astype(jnp.bfloat16)
            at = pl.ds(place * part, part)
            totals[at, pl.ds(0, LANES)] = high
            totals[at, pl.ds(LANES, LANES)] = low

    def three(c, i, carry):
        for k in range(3):
            slopes(c, 3 * i + k)
        return carry

    for t in range(len(row_peers) + 1):
        mixed[t, pl.ds(0, SUB), :] = jnp.zeros((SUB, LANES), jnp.float32)
    lines = [(2 * LANES * i, 2 * LANES) for i in range(tiles - 1)] + [(2 * LANES * (tiles - 1), 3 * LANES)]
    sum_copies = []
    for i, c in enumerate(stages):
        if c:
            for copy in row_copies[c]:
                copy.wait_recv()
        if c == 1:
            mix(*chunks[0])
        if c == 0:
            for copy in col_copies[0]:
                copy.wait_recv()
            mix(0, PAD)
            mix(PAD, PAD + SUB)
        else:
            mix(*chunks[c])
        if c == tiles - 1:
            for copy in col_copies[1]:
                copy.wait_recv()
            mix(PAD + cols, 2 * PAD + cols)
        sum_copies.append([])
        edges = [0, DIRS - 1] if i < tiles - 1 else [0, SUB // 2, DIRS - 1]
        for n, (low, high) in enumerate(zip(edges[:-1], edges[1:])):
            last = i == tiles - 1 and high == DIRS - 1
            for d in range(low, high + 1 if last or i < tiles - 1 else high):
                slopes(c, d)
            line = pl.ds(2 * LANES * i + 2 * low // SUB * LANES, ((2 * high - 2 * low) // SUB + last) * LANES)
            parts[layer, :, line] = lax.dot_general(
                pick, totals[line, :], (((1,), (1,)), ((), ())), preferred_element_type=jnp.float32
            )
            block = parts.at[layer, :, line]
            sum_copies[i] += [
                send(block, block, ss_sem.at[k, i + n], sr_sem.at[k, i + n], peers[k]) for k in range(n_layer - 1)
            ]
    whole = {}
    for i, c in enumerate(stages):
        for copy in sum_copies[i]:
            copy.wait_recv()
        line = pl.ds(*lines[i])
        total = parts[0, :, line]
        for k in range(1, n_layer):
            total = total + parts[k, :, line]
        whole[c] = total
    lane_g = lax.broadcasted_iota(jnp.int32, (groups, LANES), 1)
    for d in range(DIRS - 1):
        for s in range(2):
            item = 2 * d + s
            first = item & (SUB - 1)
            block = None
            for c in range(tiles):
                slot = (first + c) & (SUB - 1)
                piece = whole[c][:, item // SUB * LANES : (item // SUB + 1) * LANES]
                inside = (lane_g >= slot * part) & (lane_g < (slot + 1) * part)
                block = piece if block is None else jnp.where(inside, piece, block)
            if first:
                block = pltpu.roll(block, LANES - first * part, 1)
            out[s, d] = block[:, :wide]
    block = whole[tiles - 1][:, 2 * LANES :]
    out[0, DIRS - 1] = block[:, :wide]
    out[1, DIRS - 1] = block[:, wide:]

    for copy in col_copies[0] + col_copies[1] + sum(row_copies, []) + sum(sum_copies, []):
        copy.wait_send()


def in_hbm(x):
    return pltpu.with_memory_space_constraint(x, pltpu.HBM)


def on_device(sizes, layers, wind, offsets, weights, sub_index):
    rows, cols = sub_index.shape
    tiles = cols // LANES
    groups = rows // SUB
    wide = cols // SUB
    seen = 2 if sizes[1] == 2 else 3
    deep = cols + 2 * PAD
    deep_out = (2 * tiles + 1) * LANES
    hbm = pl.BlockSpec(memory_space=pltpu.HBM)
    dma = pltpu.SemaphoreType.DMA
    return pl.pallas_call(
        functools.partial(kernel, sizes),
        out_shape=pltpu.VMEM((2, DIRS, groups, wide), jnp.float32),
        in_specs=[hbm] * 5,
        out_specs=pl.BlockSpec(memory_space=pltpu.VMEM),
        scratch_shapes=[
            pltpu.SMEM((1, 2), jnp.int32),
            pltpu.SMEM((1, 2, DIRS), jnp.int32),
            pltpu.VMEM((tiles, rows, LANES), jnp.float32),
            pltpu.VMEM(weights.shape, weights.dtype),
            pltpu.VMEM(sub_index.shape, sub_index.dtype),
            pltpu.VMEM((seen, deep, LANES), jnp.float32),
            pltpu.VMEM((seen, deep + SUB, LANES), jnp.float32),
            pltpu.VMEM((seen, deep + SPARE * SUB, LANES), jnp.float32),
            pltpu.VMEM((cols, LANES), jnp.float32),
            pltpu.VMEM((DIRS, 2, cols, LANES), jnp.float32),
            pltpu.VMEM((deep_out, 2 * LANES), jnp.bfloat16),
            pltpu.VMEM((sizes[0], groups, deep_out), jnp.float32),
            dma((tiles + 4,)),
            dma((2,)),
            dma((2,)),
            dma((seen - 1, tiles)),
            dma((seen - 1, tiles)),
            dma((seen - 1, 2)),
            dma((seen - 1, 2)),
            dma((sizes[0] - 1, tiles + 1)),
            dma((sizes[0] - 1, tiles + 1)),
            pltpu.SemaphoreType.REGULAR,
        ],
        compiler_params=pltpu.CompilerParams(
            collective_id=0, has_side_effects=True, vmem_limit_bytes=32 * 1024 * 1024
        ),
    )(in_hbm(wind), in_hbm(jnp.swapaxes(offsets, 1, 2)), in_hbm(layers), in_hbm(weights), in_hbm(sub_index))


def solution(mesh):
    sizes = (mesh.shape["layer"], mesh.shape["tx"], mesh.shape["ty"])
    placed = (
        P("layer", "tx", "ty"),
        P("layer", None),
        P("layer", None, None),
        P(None, None, "tx", "ty"),
        P("tx", "ty"),
    )
    return jax.shard_map(
        functools.partial(on_device, sizes),
        mesh=mesh, in_specs=placed, out_specs=P(None, None, "tx", "ty"), check_vma=False,
    )
```

```python
import functools

import jax
import jax.numpy as jnp
from jax import lax
from jax.experimental import pallas as pl
from jax.experimental.pallas import tpu as pltpu
from jax.sharding import PartitionSpec as P

DIRS = 9
SUB = 8
LANES = 128
PAD = 72
MESH = pl.DeviceIdType.MESH
SPARE = 6


def kernel(
    sizes, wind_in, offsets_in, layers, weights, sub_index, out, wind, offsets, raw, wraw, sub, field, mixed,
    shifted, live, wlive, totals, parts, local_sem, zs_sem, zr_sem, xs_sem, xr_sem, cs_sem, cr_sem, ss_sem, sr_sem, ready, near,
):
    n_layer, n_tx, n_ty = sizes
    rows, cols = sub_index.shape
    tiles = cols // LANES
    groups = rows // SUB
    wide = cols // SUB
    span = shifted.shape[1] // SUB
    layer = lax.axis_index("layer")
    tx = lax.axis_index("tx")
    ty = lax.axis_index("ty")
    up = {"tx": lax.rem(tx + n_tx - 1, n_tx)}
    down = {"tx": lax.rem(tx + 1, n_tx)}
    left = {"ty": lax.rem(ty + n_ty - 1, n_ty)}
    right = {"ty": lax.rem(ty + 1, n_ty)}
    peers = [{"layer": layer ^ k} for k in [*range(2, n_layer), 1]]
    row_peers = [(down, 1)] if n_tx == 2 else [(down, 1), (up, 2)]
    col_peers = [(right, cols, 0), (left, PAD, PAD + cols)]
    stages = [1, 0] + list(range(2, tiles))
    cut = [PAD, 2 * PAD] + [PAD + (c + 1) * LANES + PAD for c in range(1, tiles - 1)] + [PAD + cols]
    chunks = list(zip(cut[:-1], cut[1:]))

    barrier = pltpu.get_barrier_semaphore()
    def signal(semaphore, devices):
        for device in devices:
            pl.semaphore_signal(semaphore, inc=1, device_id=device, device_id_type=MESH)

    at_right = [right] + [{**a, **right} for a, _ in row_peers]
    at_left = [left] + [{**a, **left} for a, _ in row_peers]
    same = [device for device, _ in row_peers]
    ahead_right = ty != 0
    ahead_left = ty == 1
    signal(barrier, same)
    order = [0, tiles - 1] + list(range(1, tiles - 1))
    own = {}
    for c in order:
        own[c] = pltpu.make_async_copy(layers.at[0, :, pl.ds(c * LANES, LANES)], raw.at[c], local_sem.at[c])
        own[c].start()
    for device in peers:

        @pl.when(device["layer"] > layer)
        def _(device=device):
            signal(barrier, [device])

    @pl.when(ty != 1)
    def _():
        signal(barrier, at_left)

    @pl.when(ty == 0)
    def _():
        signal(barrier, at_right)

    local = [
        pltpu.make_async_copy(wind_in, wind, local_sem.at[tiles]),
        pltpu.make_async_copy(offsets_in, offsets, local_sem.at[tiles + 1]),
        pltpu.make_async_copy(sub_index, sub, local_sem.at[tiles + 2]),
        pltpu.make_async_copy(weights, wraw, local_sem.at[tiles + 3]),
    ]
    for copy in local:
        copy.start()

    def turn_tile(c):
        own[c].wait()
        field[0, pl.ds(PAD + c * LANES, LANES), :] = raw[c].T

    turn_tile(0)
    pl.semaphore_wait(
        barrier,
        len(same) + layer + len(at_right) * ahead_right.astype(jnp.int32) + len(at_left) * ahead_left.astype(jnp.int32),
    )

    def plan(src, dst, send_sem, recv_sem, device):
        return pltpu.make_async_remote_copy(
            src_ref=src, dst_ref=dst, send_sem=send_sem, recv_sem=recv_sem,
            device_id=device, device_id_type=MESH,
        )

    def send(*args):
        copy = plan(*args)
        copy.start()
        return copy

    col_copies = [[], []]
    for k, (b, start, end) in enumerate(col_peers):
        col_copies[k].append(plan(
            field.at[0, pl.ds(start, PAD), :], field.at[0, pl.ds(end, PAD), :], zs_sem.at[k], zr_sem.at[k], b,
        ))
        for j, (a, slot) in enumerate(row_peers):
            col_copies[k].append(plan(
                field.at[k * slot, pl.ds(start, PAD), :], field.at[slot, pl.ds(end, PAD), :],
                cs_sem.at[j, k], cr_sem.at[j, k], b if k else {**a, **b},
            ))

    def start_all(copies):
        for copy in copies:
            copy.start()

    def send_rows(c):
        start, end = chunks[c]
        return [
            send(
                field.at[0, pl.ds(start, end - start), :], field.at[slot, pl.ds(start, end - start), :],
                xs_sem.at[j, c], xr_sem.at[j, c], a,
            ) for j, (a, slot) in enumerate(row_peers)
        ]

    row_copies = [send_rows(0)]
    turn_tile(tiles - 1)

    for device in peers:

        @pl.when(device["layer"] < layer)
        def _(device=device):
            signal(near, [device])

    @pl.when(ahead_right)
    def _():
        signal(ready, [right])
        start_all(col_copies[0])

    @pl.when(ahead_left)
    def _():
        signal(ready, at_left)

    for c in range(1, tiles):
        if c < tiles - 1:
            for t in range(1 if c == 1 else c + 1, c + 2):
                if t < tiles - 1:
                    turn_tile(t)
        row_copies.append(send_rows(c))

    for copy in local:
        copy.wait()
    qrow = lax.shift_right_arithmetic(wind[0, 0], 6)
    qcol = lax.shift_right_arithmetic(wind[0, 1], 6)
    frow = (wind[0, 0] - 64 * qrow).astype(jnp.float32) / 64.0
    fcol = (wind[0, 1] - 64 * qcol).astype(jnp.float32) / 64.0

    def prepare(c, i, carry):
        for k in range(3):
            d = 3 * i + k
            turn = (offsets[0, 0, d] - qrow) & (LANES - 1)
            for s in range(2):
                w = wraw[d, s, :, pl.ds(c * LANES, LANES)].T.astype(jnp.float32)
                w = pltpu.roll(w * live[pl.ds(c * LANES, LANES), :], turn, 1)
                for g in range(LANES // SUB):
                    wlive[d, s, pl.ds(c * (LANES // SUB) + g, SUB, stride=wide), :] = w[g * SUB : (g + 1) * SUB]
        return carry

    def prepare_all(c):
        live[pl.ds(c * LANES, LANES), :] = (sub[:, pl.ds(c * LANES, LANES)] >= 0).astype(jnp.float32).T
        lax.fori_loop(0, DIRS // 3, functools.partial(prepare, c), 0)

    for c in stages[:2]:
        prepare_all(c)

    @pl.when(ty != 1)
    def _():
        pl.semaphore_wait(ready, 1 + len(at_right) * (ty == 0).astype(jnp.int32))

    @pl.when(ty == 0)
    def _():
        start_all(col_copies[0])

    col_copies[1][0].start()
    for copy in row_copies[0]:
        copy.wait_recv()
    start_all(col_copies[1][1:])
    for c in stages[2:]:
        prepare_all(c)

    def mix(start, end):
        for at in range(start, end, SUB):
            mix_group(at)

    def mix_group(start):
        size = SUB
        lane = lax.broadcasted_iota(jnp.int32, (size, LANES), 1)
        here = [field[t, pl.ds(start, size), :] for t in range(len(row_peers) + 1)]
        turned = [pltpu.roll(h, 1, 1) for h in here]
        if n_tx == 2:
            before = [jnp.where(lane == 0, turned[1], turned[0]), jnp.where(lane == 0, turned[0], turned[1])]
        else:
            before = [
                jnp.where(lane == 0, turned[1], turned[0]), turned[1], jnp.where(lane == 0, turned[0], turned[2]),
            ]
        for t, (h, b) in enumerate(zip(here, before)):
            mixed[t, pl.ds(SUB + start, size), :] = (1.0 - frow) * h + frow * b
        for t in range(len(here)):
            for g in range(size // SUB):
                one = mixed[t, pl.ds(SUB + start + g * SUB, SUB), :]
                two = mixed[t, pl.ds(SUB - 1 + start + g * SUB, SUB), :]
                shifted[t, pl.ds(start // SUB + g, SUB, stride=span), :] = (1.0 - fcol) * one + fcol * two

    part = LANES // SUB
    lane_w = lax.broadcasted_iota(jnp.int32, (part, LANES), 1)
    pick_row = lax.broadcasted_iota(jnp.int32, (groups, 2 * LANES), 0)
    pick_col = lax.broadcasted_iota(jnp.int32, (groups, 2 * LANES), 1)
    pick = (lax.shift_right_logical(pick_col & (LANES - 1), 3) == pick_row).astype(jnp.bfloat16)

    def slopes(c, d):
        turn = offsets[0, 0, d] - qrow
        top = offsets[0, 1, d] - qcol + PAD
        inside = (lane_w >= turn) & (lane_w < LANES + turn)
        sums = [None, None]
        for r in range(SUB):
            start = ((top + r) & (SUB - 1)) * span + lax.shift_right_arithmetic(top + r, 3) + c * part
            seen = [shifted[t, pl.ds(start, part), :] for t in range(len(row_peers) + 1)]
            other = seen[1] if n_tx == 2 else jnp.where(lane_w < turn, seen[2], seen[1])
            view = jnp.where(inside, seen[0], other)
            for s in range(2):
                term = wlive[d, s, pl.ds(r * wide + c * part, part), :] * view
                sums[s] = term if r == 0 else sums[s] + term
        for s in range(2):
            item = 2 * d + s
            place = 2 * SUB * stages.index(c) + (item & SUB) + ((item + c) & (SUB - 1)) + (SUB if c == stages[-1] else 0)
            if d == DIRS - 1:
                place = 2 * SUB * (tiles - 1) + s * tiles + c
            back = pltpu.roll(sums[s], (-turn) & (LANES - 1), 1)
            high = back.astype(jnp.bfloat16)
            low = (back - high.astype(jnp.float32)).astype(jnp.bfloat16)
            at = pl.ds(place * part, part)
            totals[at, pl.ds(0, LANES)] = high
            totals[at, pl.ds(LANES, LANES)] = low

    def three(c, i, carry):
        for k in range(3):
            slopes(c, 3 * i + k)
        return carry

    for t in range(len(row_peers) + 1):
        mixed[t, pl.ds(0, SUB), :] = jnp.zeros((SUB, LANES), jnp.float32)
    lines = [(2 * LANES * i, 2 * LANES) for i in range(tiles - 1)] + [(2 * LANES * (tiles - 1), 3 * LANES)]
    @pl.when(layer < n_layer - 1)
    def _():
        pl.semaphore_wait(near, n_layer - 1 - layer)

    sum_copies = []
    for i, c in enumerate(stages):
        if c:
            for copy in row_copies[c]:
                copy.wait_recv()
        if c == 1:
            mix(*chunks[0])
        if c == 0:
            for copy in col_copies[0]:
                copy.wait_recv()
            mix(0, PAD)
            mix(PAD, PAD + SUB)
        else:
            mix(*chunks[c])
        if c == tiles - 1:
            for copy in col_copies[1]:
                copy.wait_recv()
            mix(PAD + cols, 2 * PAD + cols)
        sum_copies.append([])
        every = list(range(DIRS - 1))
        halves = [every[: SUB // 2] + [DIRS - 1], every[SUB // 2 :]] if i == tiles - 1 else [every + [DIRS - 1]]
        begin = 2 * LANES * i
        for n, half in enumerate(halves):
            for d in half:
                slopes(c, d)
            size = LANES if n else 2 * LANES
            line = pl.ds(begin, size)
            begin += size
            parts[layer, :, line] = lax.dot_general(
                pick, totals[line, :], (((1,), (1,)), ((), ())), preferred_element_type=jnp.float32
            )
            block = parts.at[layer, :, line]
            sum_copies[i] += [
                send(block, block, ss_sem.at[k, i + n], sr_sem.at[k, i + n], peers[k]) for k in range(n_layer - 1)
            ]
    for copy in col_copies[0] + col_copies[1] + sum(row_copies, []) + sum(sum_copies[:-1], []):
        copy.wait_send()
    whole = {}
    for i, c in enumerate(stages):
        for copy in sum_copies[i]:
            copy.wait_recv()
        line = pl.ds(*lines[i])
        total = parts[0, :, line]
        for k in range(1, n_layer):
            total = total + parts[k, :, line]
        whole[c] = total
    lane_g = lax.broadcasted_iota(jnp.int32, (groups, LANES), 1)
    for d in range(DIRS - 1):
        for s in range(2):
            item = 2 * d + s
            first = item & (SUB - 1)
            block = None
            for c in range(tiles):
                slot = (first + c) & (SUB - 1)
                tile = item // SUB + (c == stages[-1])
                piece = whole[c][:, tile * LANES : (tile + 1) * LANES]
                inside = (lane_g >= slot * part) & (lane_g < (slot + 1) * part)
                block = piece if block is None else jnp.where(inside, piece, block)
            if first:
                block = pltpu.roll(block, LANES - first * part, 1)
            out[s, d] = block[:, :wide]
    block = whole[tiles - 1][:, :LANES]
    out[0, DIRS - 1] = block[:, :wide]
    out[1, DIRS - 1] = block[:, wide:]

    for copy in sum_copies[-1]:
        copy.wait_send()


def in_hbm(x):
    return pltpu.with_memory_space_constraint(x, pltpu.HBM)


def on_device(sizes, layers, wind, offsets, weights, sub_index):
    rows, cols = sub_index.shape
    tiles = cols // LANES
    groups = rows // SUB
    wide = cols // SUB
    seen = 2 if sizes[1] == 2 else 3
    deep = cols + 2 * PAD
    deep_out = (2 * tiles + 1) * LANES
    hbm = pl.BlockSpec(memory_space=pltpu.HBM)
    dma = pltpu.SemaphoreType.DMA
    return pl.pallas_call(
        functools.partial(kernel, sizes),
        out_shape=pltpu.VMEM((2, DIRS, groups, wide), jnp.float32),
        in_specs=[hbm] * 5,
        out_specs=pl.BlockSpec(memory_space=pltpu.VMEM),
        scratch_shapes=[
            pltpu.SMEM((1, 2), jnp.int32),
            pltpu.SMEM((1, 2, DIRS), jnp.int32),
            pltpu.VMEM((tiles, rows, LANES), jnp.float32),
            pltpu.VMEM(weights.shape, weights.dtype),
            pltpu.VMEM(sub_index.shape, sub_index.dtype),
            pltpu.VMEM((seen, deep, LANES), jnp.float32),
            pltpu.VMEM((seen, deep + SUB, LANES), jnp.float32),
            pltpu.VMEM((seen, deep + SPARE * SUB, LANES), jnp.float32),
            pltpu.VMEM((cols, LANES), jnp.float32),
            pltpu.VMEM((DIRS, 2, cols, LANES), jnp.float32),
            pltpu.VMEM((deep_out, 2 * LANES), jnp.bfloat16),
            pltpu.VMEM((sizes[0], groups, deep_out), jnp.float32),
            dma((tiles + 4,)),
            dma((2,)),
            dma((2,)),
            dma((seen - 1, tiles)),
            dma((seen - 1, tiles)),
            dma((seen - 1, 2)),
            dma((seen - 1, 2)),
            dma((sizes[0] - 1, tiles + 1)),
            dma((sizes[0] - 1, tiles + 1)),
            pltpu.SemaphoreType.REGULAR,
            pltpu.SemaphoreType.REGULAR,
        ],
        compiler_params=pltpu.CompilerParams(
            collective_id=0, has_side_effects=True, vmem_limit_bytes=32 * 1024 * 1024
        ),
    )(in_hbm(wind), in_hbm(jnp.swapaxes(offsets, 1, 2)), in_hbm(layers), in_hbm(weights), in_hbm(sub_index))


def solution(mesh):
    sizes = (mesh.shape["layer"], mesh.shape["tx"], mesh.shape["ty"])
    placed = (
        P("layer", "tx", "ty"),
        P("layer", None),
        P("layer", None, None),
        P(None, None, "tx", "ty"),
        P("tx", "ty"),
    )
    return jax.shard_map(
        functools.partial(on_device, sizes),
        mesh=mesh, in_specs=placed, out_specs=P(None, None, "tx", "ty"), check_vma=False,
    )
```

```python
import functools

import jax
import jax.numpy as jnp
from jax import lax
from jax.experimental import pallas as pl
from jax.experimental.pallas import tpu as pltpu
from jax.sharding import PartitionSpec as P

DIRS = 9
SUB = 8
LANES = 128
PAD = 72
MESH = pl.DeviceIdType.MESH
SPARE = 6


def kernel(
    sizes, wind_in, offsets_in, layers, weights, sub_index, out, wind, offsets, raw, wraw, sub, field, mixed,
    shifted, live, wlive, totals, parts, local_sem, zs_sem, zr_sem, xs_sem, xr_sem, cs_sem, cr_sem, ss_sem, sr_sem, ready, near,
):
    n_layer, n_tx, n_ty = sizes
    rows, cols = sub_index.shape
    tiles = cols // LANES
    groups = rows // SUB
    wide = cols // SUB
    span = shifted.shape[1] // SUB
    layer = lax.axis_index("layer")
    tx = lax.axis_index("tx")
    ty = lax.axis_index("ty")
    up = {"tx": lax.rem(tx + n_tx - 1, n_tx)}
    down = {"tx": lax.rem(tx + 1, n_tx)}
    left = {"ty": lax.rem(ty + n_ty - 1, n_ty)}
    right = {"ty": lax.rem(ty + 1, n_ty)}
    peers = [{"layer": layer ^ k} for k in [*range(2, n_layer), 1]]
    row_peers = [(down, 1)] if n_tx == 2 else [(down, 1), (up, 2)]
    col_peers = [(right, cols, 0), (left, PAD, PAD + cols)]
    stages = [1, 0] + list(range(2, tiles))
    cut = [PAD, 2 * PAD] + [PAD + (c + 1) * LANES + PAD for c in range(1, tiles - 1)] + [PAD + cols]
    chunks = list(zip(cut[:-1], cut[1:]))

    barrier = pltpu.get_barrier_semaphore()
    def signal(semaphore, devices):
        for device in devices:
            pl.semaphore_signal(semaphore, inc=1, device_id=device, device_id_type=MESH)

    at_right = [right] + [{**a, **right} for a, _ in row_peers]
    at_left = [left] + [{**a, **left} for a, _ in row_peers]
    same = [device for device, _ in row_peers]
    ahead_right = ty != 0
    ahead_left = ty == 1
    signal(barrier, same)
    order = [0, tiles - 1] + list(range(1, tiles - 1))
    own = {}
    for c in order:
        own[c] = pltpu.make_async_copy(layers.at[0, :, pl.ds(c * LANES, LANES)], raw.at[c], local_sem.at[c])
        own[c].start()
    for device in peers:

        @pl.when(device["layer"] > layer)
        def _(device=device):
            signal(barrier, [device])

    @pl.when(ty != 1)
    def _():
        signal(barrier, at_left)

    @pl.when(ty == 0)
    def _():
        signal(barrier, at_right)

    local = [
        pltpu.make_async_copy(wind_in, wind, local_sem.at[tiles]),
        pltpu.make_async_copy(offsets_in, offsets, local_sem.at[tiles + 1]),
        pltpu.make_async_copy(sub_index, sub, local_sem.at[tiles + 2]),
        pltpu.make_async_copy(weights, wraw, local_sem.at[tiles + 3]),
    ]
    for copy in local:
        copy.start()

    def turn_tile(c):
        own[c].wait()
        field[0, pl.ds(PAD + c * LANES, LANES), :] = raw[c].T

    turn_tile(0)
    pl.semaphore_wait(
        barrier,
        len(same) + layer + len(at_right) * ahead_right.astype(jnp.int32) + len(at_left) * ahead_left.astype(jnp.int32),
    )

    def plan(src, dst, send_sem, recv_sem, device):
        return pltpu.make_async_remote_copy(
            src_ref=src, dst_ref=dst, send_sem=send_sem, recv_sem=recv_sem,
            device_id=device, device_id_type=MESH,
        )

    def send(*args):
        copy = plan(*args)
        copy.start()
        return copy

    col_copies = [[], []]
    for k, (b, start, end) in enumerate(col_peers):
        col_copies[k].append(plan(
            field.at[0, pl.ds(start, PAD), :], field.at[0, pl.ds(end, PAD), :], zs_sem.at[k], zr_sem.at[k], b,
        ))
        for j, (a, slot) in enumerate(row_peers):
            col_copies[k].append(plan(
                field.at[k * slot, pl.ds(start, PAD), :], field.at[slot, pl.ds(end, PAD), :],
                cs_sem.at[j, k], cr_sem.at[j, k], b if k else {**a, **b},
            ))

    def start_all(copies):
        for copy in copies:
            copy.start()

    def send_rows(c):
        start, end = chunks[c]
        return [
            send(
                field.at[0, pl.ds(start, end - start), :], field.at[slot, pl.ds(start, end - start), :],
                xs_sem.at[j, c], xr_sem.at[j, c], a,
            ) for j, (a, slot) in enumerate(row_peers)
        ]

    row_copies = [send_rows(0)]
    turn_tile(tiles - 1)

    for device in peers:

        @pl.when(device["layer"] < layer)
        def _(device=device):
            signal(near, [device])

    @pl.when(ahead_right)
    def _():
        signal(ready, [right])
        start_all(col_copies[0])

    @pl.when(ahead_left)
    def _():
        signal(ready, at_left)

    for c in range(1, tiles):
        if c < tiles - 1:
            for t in range(1 if c == 1 else c + 1, c + 2):
                if t < tiles - 1:
                    turn_tile(t)
        row_copies.append(send_rows(c))

    for copy in local:
        copy.wait()
    qrow = lax.shift_right_arithmetic(wind[0, 0], 6)
    qcol = lax.shift_right_arithmetic(wind[0, 1], 6)
    frow = (wind[0, 0] - 64 * qrow).astype(jnp.float32) / 64.0
    fcol = (wind[0, 1] - 64 * qcol).astype(jnp.float32) / 64.0

    def prepare(c, i, carry):
        for k in range(3):
            d = 3 * i + k
            turn = (offsets[0, 0, d] - qrow) & (LANES - 1)
            for s in range(2):
                w = wraw[d, s, :, pl.ds(c * LANES, LANES)].T.astype(jnp.float32)
                w = pltpu.roll(w * live[pl.ds(c * LANES, LANES), :], turn, 1)
                for g in range(LANES // SUB):
                    wlive[d, s, pl.ds(c * (LANES // SUB) + g, SUB, stride=wide), :] = w[g * SUB : (g + 1) * SUB]
        return carry

    def prepare_all(c):
        live[pl.ds(c * LANES, LANES), :] = (sub[:, pl.ds(c * LANES, LANES)] >= 0).astype(jnp.float32).T
        lax.fori_loop(0, DIRS // 3, functools.partial(prepare, c), 0)

    for c in stages[:2]:
        prepare_all(c)

    @pl.when(ty != 1)
    def _():
        pl.semaphore_wait(ready, 1 + len(at_right) * (ty == 0).astype(jnp.int32))

    @pl.when(ty == 0)
    def _():
        start_all(col_copies[0])

    col_copies[1][0].start()
    for copy in row_copies[0]:
        copy.wait_recv()
    start_all(col_copies[1][1:])
    for c in stages[2:]:
        prepare_all(c)

    def mix(start, end):
        for at in range(start, end, SUB):
            mix_group(at)

    def mix_group(start):
        size = SUB
        lane = lax.broadcasted_iota(jnp.int32, (size, LANES), 1)
        here = [field[t, pl.ds(start, size), :] for t in range(len(row_peers) + 1)]
        turned = [pltpu.roll(h, 1, 1) for h in here]
        if n_tx == 2:
            before = [jnp.where(lane == 0, turned[1], turned[0]), jnp.where(lane == 0, turned[0], turned[1])]
        else:
            before = [
                jnp.where(lane == 0, turned[1], turned[0]), turned[1], jnp.where(lane == 0, turned[0], turned[2]),
            ]
        for t, (h, b) in enumerate(zip(here, before)):
            mixed[t, pl.ds(SUB + start, size), :] = (1.0 - frow) * h + frow * b
        for t in range(len(here)):
            for g in range(size // SUB):
                one = mixed[t, pl.ds(SUB + start + g * SUB, SUB), :]
                two = mixed[t, pl.ds(SUB - 1 + start + g * SUB, SUB), :]
                shifted[t, pl.ds(start // SUB + g, SUB, stride=span), :] = (1.0 - fcol) * one + fcol * two

    part = LANES // SUB
    lane_w = lax.broadcasted_iota(jnp.int32, (part, LANES), 1)
    pick_row = lax.broadcasted_iota(jnp.int32, (groups, 2 * LANES), 0)
    pick_col = lax.broadcasted_iota(jnp.int32, (groups, 2 * LANES), 1)
    pick = (lax.shift_right_logical(pick_col & (LANES - 1), 3) == pick_row).astype(jnp.bfloat16)

    def slopes(c, d):
        turn = offsets[0, 0, d] - qrow
        top = offsets[0, 1, d] - qcol + PAD
        inside = (lane_w >= turn) & (lane_w < LANES + turn)
        sums = [None, None]
        for r in range(SUB):
            start = ((top + r) & (SUB - 1)) * span + lax.shift_right_arithmetic(top + r, 3) + c * part
            seen = [shifted[t, pl.ds(start, part), :] for t in range(len(row_peers) + 1)]
            other = seen[1] if n_tx == 2 else jnp.where(lane_w < turn, seen[2], seen[1])
            view = jnp.where(inside, seen[0], other)
            for s in range(2):
                term = wlive[d, s, pl.ds(r * wide + c * part, part), :] * view
                sums[s] = term if r == 0 else sums[s] + term
        for s in range(2):
            item = 2 * d + s
            place = 2 * SUB * stages.index(c) + (item & SUB) + ((item + c) & (SUB - 1)) + (SUB if c == stages[-1] else 0)
            if d == DIRS - 1:
                place = 2 * SUB * (tiles - 1) + s * tiles + c
            back = pltpu.roll(sums[s], (-turn) & (LANES - 1), 1)
            high = back.astype(jnp.bfloat16)
            low = (back - high.astype(jnp.float32)).astype(jnp.bfloat16)
            at = pl.ds(place * part, part)
            totals[at, pl.ds(0, LANES)] = high
            totals[at, pl.ds(LANES, LANES)] = low

    def three(c, i, carry):
        for k in range(3):
            slopes(c, 3 * i + k)
        return carry

    for t in range(len(row_peers) + 1):
        mixed[t, pl.ds(0, SUB), :] = jnp.zeros((SUB, LANES), jnp.float32)
    lines = [(2 * LANES * i, 2 * LANES) for i in range(tiles - 1)] + [(2 * LANES * (tiles - 1), 3 * LANES)]
    @pl.when(layer < n_layer - 1)
    def _():
        pl.semaphore_wait(near, n_layer - 1 - layer)

    sum_copies = []
    for i, c in enumerate(stages):
        if c == tiles - 1:
            for copy in col_copies[1]:
                copy.wait_recv()
            mix(PAD + cols, 2 * PAD + cols)
        if c:
            for copy in row_copies[c]:
                copy.wait_recv()
        if c == 1:
            mix(*chunks[0])
        if c == 0:
            for copy in col_copies[0]:
                copy.wait_recv()
            mix(0, PAD)
            mix(PAD, PAD + SUB)
        else:
            mix(*chunks[c])
        if c == tiles - 1:
            mix(PAD + cols, PAD + cols + SUB)
        sum_copies.append([])
        every = list(range(DIRS - 1))
        halves = [every[: SUB // 2] + [DIRS - 1], every[SUB // 2 :]] if i == tiles - 1 else [every + [DIRS - 1]]
        begin = 2 * LANES * i
        for n, half in enumerate(halves):
            for d in half:
                slopes(c, d)
            size = LANES if n else 2 * LANES
            line = pl.ds(begin, size)
            begin += size
            parts[layer, :, line] = lax.dot_general(
                pick, totals[line, :], (((1,), (1,)), ((), ())), preferred_element_type=jnp.float32
            )
            block = parts.at[layer, :, line]
            sum_copies[i] += [
                send(block, block, ss_sem.at[k, i + n], sr_sem.at[k, i + n], peers[k]) for k in range(n_layer - 1)
            ]
    for copy in col_copies[0] + col_copies[1] + sum(row_copies, []) + sum(sum_copies[:-1], []):
        copy.wait_send()
    whole = {}
    for i, c in enumerate(stages):
        for copy in sum_copies[i]:
            copy.wait_recv()
        line = pl.ds(*lines[i])
        total = parts[0, :, line]
        for k in range(1, n_layer):
            total = total + parts[k, :, line]
        whole[c] = total
    lane_g = lax.broadcasted_iota(jnp.int32, (groups, LANES), 1)
    for d in range(DIRS - 1):
        for s in range(2):
            item = 2 * d + s
            first = item & (SUB - 1)
            block = None
            for c in range(tiles):
                slot = (first + c) & (SUB - 1)
                tile = item // SUB + (c == stages[-1])
                piece = whole[c][:, tile * LANES : (tile + 1) * LANES]
                inside = (lane_g >= slot * part) & (lane_g < (slot + 1) * part)
                block = piece if block is None else jnp.where(inside, piece, block)
            if first:
                block = pltpu.roll(block, LANES - first * part, 1)
            out[s, d] = block[:, :wide]
    block = whole[tiles - 1][:, :LANES]
    out[0, DIRS - 1] = block[:, :wide]
    out[1, DIRS - 1] = block[:, wide:]

    for copy in sum_copies[-1]:
        copy.wait_send()


def in_hbm(x):
    return pltpu.with_memory_space_constraint(x, pltpu.HBM)


def on_device(sizes, layers, wind, offsets, weights, sub_index):
    rows, cols = sub_index.shape
    tiles = cols // LANES
    groups = rows // SUB
    wide = cols // SUB
    seen = 2 if sizes[1] == 2 else 3
    deep = cols + 2 * PAD
    deep_out = (2 * tiles + 1) * LANES
    hbm = pl.BlockSpec(memory_space=pltpu.HBM)
    dma = pltpu.SemaphoreType.DMA
    return pl.pallas_call(
        functools.partial(kernel, sizes),
        out_shape=pltpu.VMEM((2, DIRS, groups, wide), jnp.float32),
        in_specs=[hbm] * 5,
        out_specs=pl.BlockSpec(memory_space=pltpu.VMEM),
        scratch_shapes=[
            pltpu.SMEM((1, 2), jnp.int32),
            pltpu.SMEM((1, 2, DIRS), jnp.int32),
            pltpu.VMEM((tiles, rows, LANES), jnp.float32),
            pltpu.VMEM(weights.shape, weights.dtype),
            pltpu.VMEM(sub_index.shape, sub_index.dtype),
            pltpu.VMEM((seen, deep, LANES), jnp.float32),
            pltpu.VMEM((seen, deep + SUB, LANES), jnp.float32),
            pltpu.VMEM((seen, deep + SPARE * SUB, LANES), jnp.float32),
            pltpu.VMEM((cols, LANES), jnp.float32),
            pltpu.VMEM((DIRS, 2, cols, LANES), jnp.float32),
            pltpu.VMEM((deep_out, 2 * LANES), jnp.bfloat16),
            pltpu.VMEM((sizes[0], groups, deep_out), jnp.float32),
            dma((tiles + 4,)),
            dma((2,)),
            dma((2,)),
            dma((seen - 1, tiles)),
            dma((seen - 1, tiles)),
            dma((seen - 1, 2)),
            dma((seen - 1, 2)),
            dma((sizes[0] - 1, tiles + 1)),
            dma((sizes[0] - 1, tiles + 1)),
            pltpu.SemaphoreType.REGULAR,
            pltpu.SemaphoreType.REGULAR,
        ],
        compiler_params=pltpu.CompilerParams(
            collective_id=0, has_side_effects=True, vmem_limit_bytes=32 * 1024 * 1024
        ),
    )(in_hbm(wind), in_hbm(jnp.swapaxes(offsets, 1, 2)), in_hbm(layers), in_hbm(weights), in_hbm(sub_index))


def solution(mesh):
    sizes = (mesh.shape["layer"], mesh.shape["tx"], mesh.shape["ty"])
    placed = (
        P("layer", "tx", "ty"),
        P("layer", None),
        P("layer", None, None),
        P(None, None, "tx", "ty"),
        P("tx", "ty"),
    )
    return jax.shard_map(
        functools.partial(on_device, sizes),
        mesh=mesh, in_specs=placed, out_specs=P(None, None, "tx", "ty"), check_vma=False,
    )
```
